256 devices in a mesh: band: 16 (over x, y_lo, core), space: 16 (over y_hi, z).
Axes of the slice: x: 4, y: 4 (y_hi: 2, y_lo: 2; y = y_hi * 2 + y_lo), z: 8, core: 2. Of those that a mesh axis runs over, the one named last changes fastest.
Arguments:
- tokens: bfloat16 [16, 2048, 768], P('band', 'space'), may hold values from -6 to 6
- cotangent: bfloat16 [16, 2048, 768], P('band', 'space'), may hold values from -6 to 6
- visible: int32 [16, 2048], replicated, may hold values 0 or 1
- tau_space: float32 [12], replicated, may hold values from 1 to 48
- tau_band: float32 [12], replicated, may hold values from 1 to 48
- w_qkv_space: bfloat16 [768, 2304], replicated, may hold values from -0.21875 to 0.21875
- w_out_space: bfloat16 [768, 768], replicated, may hold values from -0.21875 to 0.21875
- w_qkv_band: bfloat16 [768, 2304], replicated, may hold values from -0.21875 to 0.21875
- w_out_band: bfloat16 [768, 768], replicated, may hold values from -0.21875 to 0.21875
Outputs:
- mixed: float32 [16, 2048, 768], P('band', 'space')
- input_grad: float32 [16, 2048, 768], P('band', 'space')
The draws below stay inside these ranges and needn't reach their ends.
All inputs are finite; a program needn't handle non-finite values.
Results may differ from the reference program's by a relative error of at most 0.038.
Values may be sent and summed in bfloat16 or wider, within the bound.
A program may use at most 128 MiB of HBM per device.

```python
import jax
import jax.numpy as jnp
from jax import lax

D = 768
HEADS = 12
HEAD_DIM = 64
T_DEV = 128
RADIUS = 64
GROUPS = 16
POSITIONS = 2048


def draw_tau_space(key, part):
    key = jax.random.fold_in(key, 11)
    key_level = jax.random.fold_in(key, 2)
    level = jax.random.uniform(key_level, (HEADS,), jnp.float32)
    return jnp.exp(jnp.log(8.0) * level)


def draw_tau_band(key, part):
    key = jax.random.fold_in(key, 12)
    key_level = jax.random.fold_in(key, 2)
    level = jax.random.uniform(key_level, (HEADS,), jnp.float32)
    return jnp.exp(jnp.log(8.0) * level)


def set_ends(drawn, stream_key, low, high):
    longest = drawn.shape.index(max(drawn.shape))
    spots = []
    for shift in (0, 1):
        where = [jax.random.randint(jax.random.fold_in(stream_key, axis), (), 0, length) for axis, length in enumerate(drawn.shape)]
        where[longest] = (where[longest] + shift) % drawn.shape[longest]
        spots.append(tuple(where))
    return drawn.at[spots[0]].set(low).at[spots[1]].set(high)


def level_of(stream_key, dims, cuts, least, high):
    def one(axis_at, shards_of):
        draws = jax.random.uniform(jax.random.fold_in(jax.random.fold_in(stream_key, 6), axis_at), (shards_of,), jnp.float32, least / len(cuts), high / len(cuts))
        return jnp.repeat(jnp.exp(draws), dims[axis_at] // shards_of).reshape((-1,) + (1,) * (len(dims) - axis_at - 1))

    gain = one(*cuts[0])
    for cut in cuts[1:]:
        gain = gain * one(*cut)
    return gain


def centred(own_key, extent, scale, bound, shards=(), kind=jnp.bfloat16):
    values = scale * jax.random.normal(own_key, extent, jnp.float32)
    if shards:
        values = values * level_of(own_key, extent, shards, -0.22, 0.18)
    return jnp.clip(values, -bound, bound).astype(kind)


def setup_inputs(seed: int = 0) -> dict:
    key_of = jax.random.split(jax.random.key(seed), 10)
    tokens = centred(key_of[0], (GROUPS, POSITIONS, D), 1.0, 6.0, ((0, 16), (1, 16)))
    cotangent = centred(key_of[1], (GROUPS, POSITIONS, D), 1.0, 6.0, ((0, 16), (1, 16)))
    visible = set_ends((jax.random.randint(key_of[2], (GROUPS, POSITIONS), 0, 4) < 1).astype(jnp.int32), jax.random.fold_in(key_of[2], 1), 0, 1)
    tau_space = draw_tau_space(jax.random.fold_in(key_of[9], 71), 0)
    tau_band = draw_tau_band(jax.random.fold_in(key_of[9], 71), 0)
    w_qkv_space = centred(key_of[5], (D, 3 * D), D ** -0.5, 0.21875)
    w_out_space = centred(key_of[6], (D, D), D ** -0.5, 0.21875)
    w_qkv_band = centred(key_of[7], (D, 3 * D), D ** -0.5, 0.21875)
    w_out_band = centred(key_of[8], (D, D), D ** -0.5, 0.21875)
    return dict(tokens=tokens, cotangent=cotangent, visible=visible, tau_space=tau_space, tau_band=tau_band, w_qkv_space=w_qkv_space, w_out_space=w_out_space, w_qkv_band=w_qkv_band, w_out_band=w_out_band)


EPS = 1e-06
NEG_FILL = -1e+30

def to_bf16(tensor):
    return lax.optimization_barrier(tensor.astype(jnp.bfloat16))

def row_norm(values):
    factor = lax.rsqrt(lax.optimization_barrier(jnp.mean(values * values, axis=-1, keepdims=True)) + EPS)
    return (values * factor, factor)

def split_heads(tensor):
    return tensor.reshape(tensor.shape[:-1] + (HEADS, HEAD_DIM))

def head_norm(tensor):
    pieces = split_heads(tensor)
    factor = lax.rsqrt(lax.optimization_barrier(jnp.mean(pieces * pieces, axis=-1, keepdims=True)) + EPS)
    return (pieces * factor, factor)

def norm_back(unit, factor, upstream):
    return factor * (upstream - unit * lax.optimization_barrier(jnp.mean(unit * upstream, axis=-1, keepdims=True)))

def flat_dot(left, right):
    leading = left.shape[:-1]
    result = jnp.dot(left.reshape(-1, left.shape[-1]), right, preferred_element_type=jnp.float32)
    return result.reshape(leading + (right.shape[-1],))

def projections(normed, w_qkv):
    mixed_qkv = flat_dot(normed, w_qkv)
    query_unit, query_factor = head_norm(mixed_qkv[..., :D])
    key_unit, key_factor = head_norm(mixed_qkv[..., D:2 * D])
    return (query_unit, query_factor, key_unit, key_factor, split_heads(mixed_qkv[..., 2 * D:]))

def softmax_masked(scores, allowed):
    scores = jnp.where(allowed, scores, NEG_FILL)
    largest = lax.optimization_barrier(jnp.max(scores, axis=-1, keepdims=True))
    weights = jnp.where(allowed, jnp.exp(scores - largest), 0.0)
    return to_bf16(weights / lax.optimization_barrier(jnp.sum(weights, axis=-1, keepdims=True)))

def wrap_pad(tensor):
    return jnp.concatenate([tensor[POSITIONS - RADIUS:], tensor, tensor[:RADIUS]], axis=0)

def fold_pad(padded):
    middle = padded[RADIUS:RADIUS + POSITIONS]
    middle = middle.at[POSITIONS - RADIUS:].add(padded[:RADIUS])
    return middle.at[:RADIUS].add(padded[POSITIONS + RADIUS:])

def window_weights(query_blk, key_blk, vis_blk, tau):
    query_count = query_blk.shape[0]
    offset = jnp.arange(query_count + 2 * RADIUS, dtype=jnp.int32)[None, :] - jnp.arange(query_count, dtype=jnp.int32)[:, None]
    allowed = (offset >= 0) & (offset <= 2 * RADIUS) & ((vis_blk[None, :] == 1) | (offset == RADIUS))
    scores = jnp.einsum('ihd,jhd->hij', query_blk.astype(jnp.float32), key_blk.astype(jnp.float32)) * (tau / HEAD_DIM)[:, None, None]
    return softmax_masked(scores, allowed[None])

def window_forward(query_grp, key_grp, value_grp, vis_grp, tau):
    key_pad = wrap_pad(key_grp)
    value_pad = wrap_pad(value_grp)
    vis_pad = wrap_pad(vis_grp)
    key_span = T_DEV + 2 * RADIUS

    def one_block(block_id):
        offset = block_id * T_DEV
        weights = window_weights(lax.dynamic_slice_in_dim(query_grp, offset, T_DEV, 0), lax.dynamic_slice_in_dim(key_pad, offset, key_span, 0), lax.dynamic_slice_in_dim(vis_pad, offset, key_span, 0), tau)
        value_blk = lax.dynamic_slice_in_dim(value_pad, offset, key_span, 0)
        return to_bf16(jnp.einsum('hij,jhd->ihd', weights.astype(jnp.float32), value_blk.astype(jnp.float32)))
    result = lax.map(one_block, jnp.arange(POSITIONS // T_DEV, dtype=jnp.int32))
    return result.reshape(POSITIONS, HEADS, HEAD_DIM)

def window_backward(query_grp, key_grp, value_grp, vis_grp, upstream, tau):
    key_pad = wrap_pad(key_grp)
    value_pad = wrap_pad(value_grp)
    vis_pad = wrap_pad(vis_grp)
    key_span = T_DEV + 2 * RADIUS

    def one_block(carry, block_id):
        grad_key, grad_value = carry
        offset = block_id * T_DEV
        query_blk = lax.dynamic_slice_in_dim(query_grp, offset, T_DEV, 0)
        upstream_blk = lax.dynamic_slice_in_dim(upstream, offset, T_DEV, 0).astype(jnp.float32)
        key_blk = lax.dynamic_slice_in_dim(key_pad, offset, key_span, 0)
        value_blk = lax.dynamic_slice_in_dim(value_pad, offset, key_span, 0).astype(jnp.float32)
        weights = window_weights(query_blk, key_blk, lax.dynamic_slice_in_dim(vis_pad, offset, key_span, 0), tau)
        weight_f = weights.astype(jnp.float32)
        dot_weights = jnp.einsum('ihd,jhd->hij', upstream_blk, value_blk)
        row_dot = lax.optimization_barrier(jnp.sum(weight_f * dot_weights, axis=-1, keepdims=True))
        dscore = to_bf16(weight_f * (dot_weights - row_dot) * (tau / HEAD_DIM)[:, None, None]).astype(jnp.float32)
        grad_query = jnp.einsum('hij,jhd->ihd', dscore, key_blk.astype(jnp.float32))
        key_part = jnp.einsum('hij,ihd->jhd', dscore, query_blk.astype(jnp.float32))
        value_part = jnp.einsum('hij,ihd->jhd', weight_f, upstream_blk)
        grad_key = lax.dynamic_update_slice_in_dim(grad_key, lax.dynamic_slice_in_dim(grad_key, offset, key_span, 0) + key_part, offset, 0)
        grad_value = lax.dynamic_update_slice_in_dim(grad_value, lax.dynamic_slice_in_dim(grad_value, offset, key_span, 0) + value_part, offset, 0)
        return ((grad_key, grad_value), grad_query)
    zero_pad = jnp.zeros((POSITIONS + 2 * RADIUS, HEADS, HEAD_DIM), jnp.float32)
    (grad_key, grad_value), grad_query = lax.scan(one_block, (zero_pad, zero_pad), jnp.arange(POSITIONS // T_DEV, dtype=jnp.int32))
    return (grad_query.reshape(POSITIONS, HEADS, HEAD_DIM), fold_pad(grad_key), fold_pad(grad_value))

def cross_weights(query_grp, key_float, allowed, tau):
    scores = jnp.einsum('thd,gthd->thg', query_grp.astype(jnp.float32), key_float) * (tau / HEAD_DIM)[None, :, None]
    return softmax_masked(scores, allowed[:, None, :])

def reference(tokens, cotangent, visible, tau_space, tau_band, w_qkv_space, w_out_space, w_qkv_band, w_out_band):
    inputs = tokens.astype(jnp.float32)
    normed_one_unit, normed_one_factor = row_norm(inputs)
    normed_one = to_bf16(normed_one_unit)
    query_one_unit, query_one_factor, key_one_unit, key_one_factor, value_one_raw = projections(normed_one, w_qkv_space)
    query_one = to_bf16(query_one_unit)
    key_one = to_bf16(key_one_unit)
    value_one = to_bf16(value_one_raw)

    def forward_group(packed):
        return window_forward(packed[0], packed[1], packed[2], packed[3], tau_space)
    attended_one = lax.map(forward_group, (query_one, key_one, value_one, visible))
    after_one = to_bf16(inputs + flat_dot(attended_one.reshape(GROUPS, POSITIONS, D), w_out_space))
    after_float = after_one.astype(jnp.float32)
    normed_two_unit, normed_two_factor = row_norm(after_float)
    normed_two = to_bf16(normed_two_unit)
    query_two_unit, query_two_factor, key_two_unit, key_two_factor, value_two_raw = projections(normed_two, w_qkv_band)
    query_two = to_bf16(query_two_unit)
    key_float = to_bf16(key_two_unit).astype(jnp.float32)
    value_float = to_bf16(value_two_raw).astype(jnp.float32)
    group_ids = jnp.arange(GROUPS, dtype=jnp.int32)
    visible_cols = visible.T == 1

    def allowed_for(group_id):
        return visible_cols | (group_ids[None, :] == group_id)

    def forward_cross(group_id):
        query_grp = lax.dynamic_index_in_dim(query_two, group_id, 0, keepdims=False)
        weights = cross_weights(query_grp, key_float, allowed_for(group_id), tau_band)
        return to_bf16(jnp.einsum('thg,gthd->thd', weights.astype(jnp.float32), value_float))
    attended_two = lax.map(forward_cross, group_ids)
    mixed = after_float + flat_dot(attended_two.reshape(GROUPS, POSITIONS, D), w_out_band)
    grad_att_two = split_heads(to_bf16(flat_dot(cotangent, w_out_band.T)))

    def cross_step(carry, group_id):
        acc_key, acc_value = carry
        query_grp = lax.dynamic_index_in_dim(query_two, group_id, 0, keepdims=False).astype(jnp.float32)
        upstream_grp = lax.dynamic_index_in_dim(grad_att_two, group_id, 0, keepdims=False).astype(jnp.float32)
        weights = cross_weights(query_grp, key_float, allowed_for(group_id), tau_band)
        weight_f = weights.astype(jnp.float32)
        dot_weights = jnp.einsum('thd,gthd->thg', upstream_grp, value_float)
        row_dot = lax.optimization_barrier(jnp.sum(weight_f * dot_weights, axis=-1, keepdims=True))
        dscore = to_bf16(weight_f * (dot_weights - row_dot) * (tau_band / HEAD_DIM)[None, :, None]).astype(jnp.float32)
        grad_query = jnp.einsum('thg,gthd->thd', dscore, key_float)
        key_part = to_bf16(jnp.einsum('thg,thd->gthd', dscore, query_grp)).astype(jnp.float32)
        value_part = to_bf16(jnp.einsum('thg,thd->gthd', weight_f, upstream_grp)).astype(jnp.float32)
        return ((acc_key + key_part, acc_value + value_part), grad_query)
    zero_all = jnp.zeros((GROUPS, POSITIONS, HEADS, HEAD_DIM), jnp.float32)
    (grad_key_two, grad_value_two), grad_query_two = lax.scan(cross_step, (zero_all, zero_all), group_ids)
    grad_qkv_two = to_bf16(jnp.concatenate([norm_back(query_two_unit, query_two_factor, grad_query_two).reshape(GROUPS, POSITIONS, D), norm_back(key_two_unit, key_two_factor, grad_key_two).reshape(GROUPS, POSITIONS, D), grad_value_two.reshape(GROUPS, POSITIONS, D)], axis=-1))
    grad_normed_two = flat_dot(grad_qkv_two, w_qkv_band.T)
    grad_after = to_bf16(cotangent.astype(jnp.float32) + norm_back(normed_two_unit, normed_two_factor, grad_normed_two))
    grad_att_one = split_heads(to_bf16(flat_dot(grad_after, w_out_space.T)))

    def backward_group(packed):
        return window_backward(packed[0], packed[1], packed[2], packed[3], packed[4], tau_space)
    grad_query_one, grad_key_one, grad_value_one = lax.map(backward_group, (query_one, key_one, value_one, visible, grad_att_one))
    grad_qkv_one = to_bf16(jnp.concatenate([norm_back(query_one_unit, query_one_factor, grad_query_one).reshape(GROUPS, POSITIONS, D), norm_back(key_one_unit, key_one_factor, grad_key_one).reshape(GROUPS, POSITIONS, D), grad_value_one.reshape(GROUPS, POSITIONS, D)], axis=-1))
    grad_normed_one = flat_dot(grad_qkv_one, w_qkv_space.T)
    input_grad = grad_after.astype(jnp.float32) + norm_back(normed_one_unit, normed_one_factor, grad_normed_one)
    return (mixed, input_grad)
```

```python
import functools

import jax
import jax.numpy as jnp
from jax import lax
from jax.experimental import pallas as pl
from jax.experimental.pallas import tpu as pltpu
from jax.sharding import PartitionSpec as P

D = 768
HALF = D // 2
HEADS = 12
HEAD_DIM = 64
PAIRS = HEADS // 2
T = 128
RADIUS = 64
EPS = 1e-06
MESH = pl.DeviceIdType.MESH
F32 = jnp.float32
BF16 = jnp.bfloat16


def dot(left, right):
    return jnp.dot(left, right, preferred_element_type=F32)


def dot_nt(left, right):
    return lax.dot_general(left, right, (((1,), (1,)), ((), ())), preferred_element_type=F32)


def dot_tn(left, right):
    return lax.dot_general(left, right, (((0,), (0,)), ((), ())), preferred_element_type=F32)


def row_factor(values):
    return lax.rsqrt(jnp.sum(values * values, axis=-1, keepdims=True) * (1.0 / D) + EPS)


def row_back(unit, factor, upstream):
    return factor * (upstream - unit * (jnp.sum(unit * upstream, axis=-1, keepdims=True) * (1.0 / D)))


def head_means(values, ones):
    low = values.astype(BF16)
    width = ones.shape[0]
    parts = [dot(low[:, at : at + width], ones) for at in range(0, values.shape[1], width)]
    return jnp.concatenate(parts, axis=1) * (1.0 / HEAD_DIM)


def head_factor(values, ones):
    return lax.rsqrt(head_means(values * values, ones) + EPS)


def head_back(unit, factor, upstream, ones):
    return factor * (upstream - unit * head_means(unit * upstream, ones))


def stacked(pair, low):
    return jnp.concatenate([jnp.where(low, pair, 0.0), jnp.where(low, 0.0, pair)], axis=0).astype(BF16)


def lanes(pair):
    return slice(pair * 128, pair * 128 + 128)


def pair_weights(query_stack, key_pair, mask, scale_a, scale_b):
    scores = dot_nt(query_stack, key_pair)
    pieces = []
    for part, scale in ((scores[:T], scale_a), (scores[T:], scale_b)):
        grown = jnp.exp(part * scale) * mask
        pieces.append(grown * (1.0 / jnp.sum(grown, axis=-1, keepdims=True)))
    return jnp.concatenate(pieces, axis=0).astype(BF16)


def pair_dscore(weights, upstream_stack, value_pair, scale_a, scale_b):
    inner = dot_nt(upstream_stack, value_pair)
    weight_f = weights.astype(F32)
    pieces = []
    for rows, scale in ((slice(0, T), scale_a), (slice(T, 2 * T), scale_b)):
        w, p = weight_f[rows], inner[rows]
        total = jnp.sum(w * p, axis=-1, keepdims=True)
        pieces.append(w * (p - total) * scale)
    return jnp.concatenate(pieces, axis=0).astype(BF16)


def kernel(
    bands,
    spaces,
    tok_hbm,
    cot_hbm,
    vis_hbm,
    tau_space,
    tau_band,
    wqs_hbm,
    wos_hbm,
    wqb_hbm,
    wob_hbm,
    mixed_ref,
    grad_ref,
    tok,
    halo,
    cot,
    vis,
    wqs,
    wos,
    wqb,
    wob,
    key_ext,
    value_ext,
    query_stack,
    weights_one,
    unit_q,
    fact_q,
    unit_k,
    fact_k,
    wide,
    after,
    grads,
    grad_kv,
    sent,
    got,
    rim_sent,
    rim_got,
    local_sem,
    halo_send,
    halo_recv,
    all_send,
    all_recv,
    rim_send,
    rim_recv,
):
    band = lax.axis_index("band")
    space = lax.axis_index("space")
    count = T // bands
    right = lax.rem(space + 1, spaces)
    left = lax.rem(space + spaces - 1, spaces)

    def local(source, target, index):
        return pltpu.make_async_copy(source, target, local_sem.at[index])

    copies = {
        "tok": local(tok_hbm.at[0], tok, 0),
        "wqs": local(wqs_hbm, wqs, 1),
        "cot": local(cot_hbm.at[0], cot, 2),
        "wos": local(wos_hbm, wos, 3),
        "wob": local(wob_hbm, wob, 4),
        "wqb": local(wqb_hbm, wqb, 5),
    }
    for index, block in enumerate((left, space, right)):
        copies["vis%d" % index] = local(
            vis_hbm.at[:, pl.ds(pl.multiple_of(block * T, T), T)], vis.at[index], 6 + index
        )
    for name in ("tok", "wqs", "cot", "vis0", "vis1", "vis2", "wos", "wob", "wqb"):
        copies[name].start()

    barrier = pltpu.get_barrier_semaphore()
    for step in range(1, bands):
        pl.semaphore_signal(
            barrier,
            inc=1,
            device_id=(lax.rem(band + step, bands), space),
            device_id_type=MESH,
        )
    for other in (left, right):
        pl.semaphore_signal(barrier, inc=1, device_id=(band, other), device_id_type=MESH)
    pl.semaphore_wait(barrier, bands + 1)

    to_right = pltpu.make_async_remote_copy(
        src_ref=tok_hbm.at[0, pl.ds(T - RADIUS, RADIUS)],
        dst_ref=halo.at[pl.ds(RADIUS, RADIUS)],
        send_sem=halo_send.at[0],
        recv_sem=halo_recv.at[0],
        device_id=(band, right),
        device_id_type=MESH,
    )
    to_left = pltpu.make_async_remote_copy(
        src_ref=tok_hbm.at[0, pl.ds(0, RADIUS)],
        dst_ref=halo.at[pl.ds(0, RADIUS)],
        send_sem=halo_send.at[1],
        recv_sem=halo_recv.at[1],
        device_id=(band, left),
        device_id_type=MESH,
    )
    to_right.start()
    to_left.start()

    def exchange(phase, step):
        other = lax.rem(band + step, bands)
        return pltpu.make_async_remote_copy(
            src_ref=sent.at[phase, other],
            dst_ref=got.at[phase, band],
            send_sem=all_send.at[phase, step],
            recv_sem=all_recv.at[phase, step],
            device_id=(other, space),
            device_id_type=MESH,
        )

    def scatter(phase, rows):
        pieces = [
            rows[:, :HALF].reshape(bands, count, HALF),
            rows[:, HALF:].reshape(bands, count, HALF),
        ]
        sent[phase] = jnp.concatenate(pieces, axis=1).astype(BF16)
        for step in range(1, bands):
            exchange(phase, step).start()
        got[phase, band] = sent[phase, band]

    def collect(phase):
        for step in range(1, bands):
            exchange(phase, step).wait_recv()
        rows = got[phase].astype(F32)
        return jnp.concatenate(
            [rows[:, :count].reshape(T, HALF), rows[:, count:].reshape(T, HALF)], axis=1
        )

    low = lax.broadcasted_iota(jnp.int32, (T, 128), 1) < HEAD_DIM
    ones = jnp.where(
        (lax.broadcasted_iota(jnp.int32, (256, 256), 0) >> 6)
        == (lax.broadcasted_iota(jnp.int32, (256, 256), 1) >> 6),
        1.0,
        0.0,
    ).astype(BF16)
    scale_space = [tau_space[head] * (1.0 / HEAD_DIM) for head in range(HEADS)]
    scale_band = [tau_band[head] * (1.0 / HEAD_DIM) for head in range(HEADS)]

    copies["cot"].wait()
    scatter(0, cot[...].astype(F32))

    for index in range(3):
        copies["vis%d" % index].wait()
    group = lax.broadcasted_iota(jnp.int32, (bands, 128), 0)
    lane = lax.broadcasted_iota(jnp.int32, (bands, 128), 1)

    def own_row(index):
        return jnp.sum(jnp.where(group == band, vis[index], 0), axis=0, keepdims=True)

    edge = lane[:1] < RADIUS
    vis_row = jnp.concatenate([own_row(1), jnp.where(edge, own_row(2), own_row(0))], axis=1)
    row = lax.broadcasted_iota(jnp.int32, (T, 2 * T), 0)
    col = lax.broadcasted_iota(jnp.int32, (T, 2 * T), 1)
    offset = jnp.where(col < T + RADIUS, col, col - 2 * T) - row
    near = (offset >= -RADIUS) & (offset <= RADIUS)
    mask_one = jnp.where(near & ((vis_row == 1) | (offset == 0)), 1.0, 0.0)
    row, col = row[:, :T], col[:, :T]
    pick = jnp.where(row == band * count + lax.rem(col, count), 1.0, 0.0)
    spread = dot(vis[1].astype(F32), pick)
    seen = jnp.sum(
        jnp.where(group == lax.div(lane, count), spread, 0.0), axis=0, keepdims=True
    )
    same = lax.rem(row, count) == lax.rem(col, count)
    mask_two = jnp.where(same & ((seen > 0.5) | (row == col)), 1.0, 0.0)

    copies["tok"].wait()
    inputs = tok[...].astype(F32)
    fact_one = row_factor(inputs)
    unit_one = inputs * fact_one
    normed = unit_one.astype(BF16)
    copies["wqs"].wait()
    raw = dot(normed, wqs[:, :D])
    factor = head_factor(raw, ones)
    unit = raw * factor
    unit_q[0] = unit
    fact_q[0] = factor
    for pair in range(PAIRS):
        query_stack[0, pair] = stacked(unit[:, lanes(pair)], low)
    raw = dot(normed, wqs[:, D : 2 * D])
    factor = head_factor(raw, ones)
    unit = raw * factor
    unit_k[0] = unit
    fact_k[0] = factor
    key_ext[:T] = unit.astype(BF16)
    value_ext[:T] = dot(normed, wqs[:, 2 * D :]).astype(BF16)

    to_right.wait_recv()
    to_left.wait_recv()
    rim = halo[...].astype(F32)
    normed = (rim * row_factor(rim)).astype(BF16)
    raw = dot(normed, wqs[:, D : 2 * D])
    key_ext[T:] = (raw * head_factor(raw, ones)).astype(BF16)
    value_ext[T:] = dot(normed, wqs[:, 2 * D :]).astype(BF16)

    for pair in range(PAIRS):
        weights = pair_weights(
            query_stack[0, pair],
            key_ext[:, lanes(pair)],
            mask_one,
            scale_space[2 * pair],
            scale_space[2 * pair + 1],
        )
        weights_one[pair] = weights
        out = dot(weights, value_ext[:, lanes(pair)])
        wide[:, lanes(pair)] = jnp.where(low, out[:T], out[T:]).astype(BF16)
    copies["wos"].wait()
    result = tok[...].astype(F32) + dot(wide[:, :D], wos[...])
    after[...] = result.astype(BF16)
    scatter(1, after[...].astype(F32))

    upstream = collect(0)
    copies["wob"].wait()
    grad_att = dot_nt(upstream.astype(BF16), wob[...])
    for pair in range(PAIRS):
        query_stack[2, pair] = stacked(grad_att[:, lanes(pair)], low)
    copies["wqb"].wait()
    rows = collect(1)
    fact_two = row_factor(rows)
    unit_two = rows * fact_two
    normed = unit_two.astype(BF16)
    raw = dot(normed, wqb[:, :D])
    factor = head_factor(raw, ones)
    unit = raw * factor
    unit_q[1] = unit
    fact_q[1] = factor
    for pair in range(PAIRS):
        query_stack[1, pair] = stacked(unit[:, lanes(pair)], low)
    raw = dot(normed, wqb[:, D : 2 * D])
    factor = head_factor(raw, ones)
    unit = raw * factor
    unit_k[1] = unit
    fact_k[1] = factor
    key_two = unit.astype(BF16)
    value_two = dot(normed, wqb[:, 2 * D :]).astype(BF16)
    attended = []
    for pair in range(PAIRS):
        scales = (scale_band[2 * pair], scale_band[2 * pair + 1])
        keys, values = key_two[:, lanes(pair)], value_two[:, lanes(pair)]
        queries, ups = query_stack[1, pair], query_stack[2, pair]
        weights = pair_weights(queries, keys, mask_two, *scales)
        out = dot(weights, values)
        attended.append(jnp.where(low, out[:T], out[T:]))
        dscore = pair_dscore(weights, ups, values, *scales)
        out = dot(dscore, keys)
        grads[:, pair * 128 : pair * 128 + 128] = jnp.where(low, out[:T], out[T:])
        grads[:, D + pair * 128 : D + pair * 128 + 128] = dot_tn(dscore, queries)
        wide[:, 2 * D + pair * 128 : 2 * D + pair * 128 + 128] = dot_tn(weights, ups).astype(BF16)
    scatter(2, jnp.concatenate(attended, axis=1))
    wide[:, :D] = head_back(unit_q[1], fact_q[1], grads[:, :D], ones).astype(BF16)
    wide[:, D : 2 * D] = head_back(unit_k[1], fact_k[1], grads[:, D:], ones).astype(BF16)
    back = dot_nt(wide[...], wqb[...])
    scatter(3, upstream + row_back(unit_two, fact_two, back))

    mixed_ref[0] = after[...].astype(F32) + dot(collect(2).astype(BF16), wob[...])
    grad_after = collect(3)
    grad_att = dot_nt(grad_after.astype(BF16), wos[...])
    for pair in range(PAIRS):
        query_stack[2, pair] = stacked(grad_att[:, lanes(pair)], low)

    def rims(pair):
        for side, other in ((0, right), (1, left)):
            yield pltpu.make_async_remote_copy(
                src_ref=rim_sent.at[pair, pl.ds(side * RADIUS, RADIUS)],
                dst_ref=rim_got.at[pair, pl.ds(side * RADIUS, RADIUS)],
                send_sem=rim_send.at[side, pair],
                recv_sem=rim_recv.at[side, pair],
                device_id=(band, other),
                device_id_type=MESH,
            )

    for pair in range(PAIRS):
        scales = (scale_space[2 * pair], scale_space[2 * pair + 1])
        keys, values = key_ext[:, lanes(pair)], value_ext[:, lanes(pair)]
        queries, ups = query_stack[0, pair], query_stack[2, pair]
        weights = weights_one[pair]
        dscore = pair_dscore(weights, ups, values, *scales)
        out = dot_tn(dscore, queries)
        grad_kv[pair, :, :128] = out[:T]
        rim_sent[pair, :, :128] = out[T:].astype(BF16)
        out = dot_tn(weights, ups)
        grad_kv[pair, :, 128:] = out[:T]
        rim_sent[pair, :, 128:] = out[T:].astype(BF16)
        for copy in rims(pair):
            copy.start()
        out = dot(dscore, keys)
        grads[:, pair * 128 : pair * 128 + 128] = jnp.where(low, out[:T], out[T:])
    wide[:, :D] = head_back(unit_q[0], fact_q[0], grads[:, :D], ones).astype(BF16)
    back = dot_nt(wide[:, :D], wqs[:, :D])
    for pair in range(PAIRS):
        for copy in rims(pair):
            copy.wait_recv()
        total = grad_kv[pair] + rim_got[pair].astype(F32)
        grads[:, D + pair * 128 : D + pair * 128 + 128] = total[:, :128]
        wide[:, 2 * D + pair * 128 : 2 * D + pair * 128 + 128] = total[:, 128:].astype(BF16)
    wide[:, D : 2 * D] = head_back(unit_k[0], fact_k[0], grads[:, D:], ones).astype(BF16)
    back = back + dot_nt(wide[:, D:], wqs[:, D:])
    inputs = tok[...].astype(F32)
    fact_one = row_factor(inputs)
    grad_ref[0] = grad_after + row_back(inputs * fact_one, fact_one, back)

    to_right.wait_send()
    to_left.wait_send()
    for phase in range(4):
        for step in range(1, bands):
            exchange(phase, step).wait_send()
    for pair in range(PAIRS):
        for copy in rims(pair):
            copy.wait_send()


def per_device(bands, spaces, *arrays):
    any_space = pl.BlockSpec(memory_space=pl.ANY)
    smem = pl.BlockSpec(memory_space=pltpu.SMEM)
    vmem = pl.BlockSpec(memory_space=pltpu.VMEM)
    out = jax.ShapeDtypeStruct((1, T, D), F32)
    count = T // bands
    dma = pltpu.SemaphoreType.DMA
    scratch = [
        pltpu.VMEM((T, D), BF16),
        pltpu.VMEM((T, D), BF16),
        pltpu.VMEM((T, D), BF16),
        pltpu.VMEM((3, bands, T), jnp.int32),
        pltpu.VMEM((D, 3 * D), BF16),
        pltpu.VMEM((D, D), BF16),
        pltpu.VMEM((D, 3 * D), BF16),
        pltpu.VMEM((D, D), BF16),
        pltpu.VMEM((2 * T, D), BF16),
        pltpu.VMEM((2 * T, D), BF16),
        pltpu.VMEM((3, PAIRS, 2 * T, 128), BF16),
        pltpu.VMEM((PAIRS, 2 * T, 2 * T), BF16),
        pltpu.VMEM((2, T, D), F32),
        pltpu.VMEM((2, T, D), F32),
        pltpu.VMEM((2, T, D), F32),
        pltpu.VMEM((2, T, D), F32),
        pltpu.VMEM((T, 3 * D), BF16),
        pltpu.VMEM((T, D), BF16),
        pltpu.VMEM((T, 2 * D), F32),
        pltpu.VMEM((PAIRS, T, 256), F32),
        pltpu.VMEM((4, bands, 2 * count, HALF), BF16),
        pltpu.VMEM((4, bands, 2 * count, HALF), BF16),
        pltpu.VMEM((PAIRS, T, 256), BF16),
        pltpu.VMEM((PAIRS, T, 256), BF16),
        dma((9,)),
        dma((2,)),
        dma((2,)),
        dma((4, bands)),
        dma((4, bands)),
        dma((2, PAIRS)),
        dma((2, PAIRS)),
    ]
    return pl.pallas_call(
        functools.partial(kernel, bands, spaces),
        out_shape=(out, out),
        in_specs=[any_space] * 3 + [smem] * 2 + [any_space] * 4,
        out_specs=(vmem, vmem),
        scratch_shapes=scratch,
        compiler_params=pltpu.CompilerParams(
            collective_id=0, has_side_effects=True, vmem_limit_bytes=48 * 1024 * 1024
        ),
        cost_estimate=pl.CostEstimate(
            flops=3_500_000_000, bytes_accessed=11_000_000, transcendentals=600_000
        ),
    )(*arrays)


def solution(mesh):
    cells = P("band", "space", None)
    return jax.shard_map(
        functools.partial(per_device, mesh.shape["band"], mesh.shape["space"]),
        mesh=mesh,
        in_specs=(cells, cells, P(), P(), P(), P(), P(), P(), P()),
        out_specs=(cells, cells),
        check_vma=False,
    )
```

```python
import functools

import jax
import jax.numpy as jnp
from jax import lax
from jax.experimental import pallas as pl
from jax.experimental.pallas import tpu as pltpu
from jax.sharding import PartitionSpec as P

D = 768
HALF = D // 2
HEADS = 12
HEAD_DIM = 64
PAIRS = HEADS // 2
T = 128
RADIUS = 64
EPS = 1e-06
MESH = pl.DeviceIdType.MESH
F32 = jnp.float32
BF16 = jnp.bfloat16


def dot(left, right):
    return jnp.dot(left, right, preferred_element_type=F32)


def dot_nt(left, right):
    return lax.dot_general(left, right, (((1,), (1,)), ((), ())), preferred_element_type=F32)


def dot_tn(left, right):
    return lax.dot_general(left, right, (((0,), (0,)), ((), ())), preferred_element_type=F32)


def row_factor(values):
    return lax.rsqrt(jnp.sum(values * values, axis=-1, keepdims=True) * (1.0 / D) + EPS)


def row_back(unit, factor, upstream):
    return factor * (upstream - unit * (jnp.sum(unit * upstream, axis=-1, keepdims=True) * (1.0 / D)))


def head_means(values, ones):
    low = values.astype(BF16)
    width = ones.shape[0]
    parts = [dot(low[:, at : at + width], ones) for at in range(0, values.shape[1], width)]
    return jnp.concatenate(parts, axis=1) * (1.0 / HEAD_DIM)


def head_factor(values, ones):
    return lax.rsqrt(head_means(values * values, ones) + EPS)


def head_back(unit, factor, upstream, ones):
    return factor * (upstream - unit * head_means(unit * upstream, ones))


def stacked(pair, low):
    return jnp.concatenate([jnp.where(low, pair, 0.0), jnp.where(low, 0.0, pair)], axis=0).astype(BF16)


def lanes(pair):
    return slice(pair * 128, pair * 128 + 128)


def paired(low, stack):
    return jnp.where(low, stack[:T], stack[T:])


def grown(query_stack, keys, mask):
    scores = jnp.exp(dot_nt(query_stack, keys))
    return jnp.concatenate([scores[:T] * mask, scores[T:] * mask], axis=0).astype(BF16)


def inner(ups, outs, values_one):
    return dot_nt(jnp.concatenate([ups, outs], axis=1), values_one)


def kernel(
    bands,
    spaces,
    tok_hbm,
    cot_hbm,
    vis_hbm,
    tau_space_hbm,
    tau_band_hbm,
    wqs_hbm,
    wos_hbm,
    wqb_hbm,
    wob_hbm,
    mixed_hbm,
    grad_hbm,
    tok,
    halo,
    cot,
    vis,
    tau_space,
    tau_band,
    wqs,
    wos,
    wqb,
    wob,
    wqs_t,
    wos_t,
    wqb_t,
    keys,
    values,
    keys_two,
    values_two,
    queries,
    ups_stack,
    grown_one,
    grown_rim,
    partial,
    inverse,
    inverse_rim,
    unit_q,
    fact_q,
    unit_k,
    fact_k,
    wide,
    after,
    attended,
    attended_rim,
    stats,
    stats_rim,
    grads,
    sent,
    got,
    got_rim,
    mixed,
    grad,
    local_sem,
    near_send,
    near_recv,
    all_send,
    all_recv,
    far_send,
    far_recv,
):
    band = lax.axis_index("band")
    space = lax.axis_index("space")
    count = T // bands
    right = lax.rem(space + 1, spaces)
    left = lax.rem(space + spaces - 1, spaces)

    def local(source, target, index):
        return pltpu.make_async_copy(source, target, local_sem.at[index])

    copies = {
        "tok": local(tok_hbm.at[0], tok, 0),
        "wqs": local(wqs_hbm, wqs, 1),
        "cot": local(cot_hbm.at[0], cot, 2),
        "wos": local(wos_hbm, wos, 3),
        "wob": local(wob_hbm, wob, 4),
        "wqb": local(wqb_hbm, wqb, 5),
        "tau_space": local(tau_space_hbm, tau_space, 9),
        "tau_band": local(tau_band_hbm, tau_band, 10),
        "mixed": local(mixed, mixed_hbm.at[0], 11),
        "grad": local(grad, grad_hbm.at[0], 12),
    }
    for index, block in enumerate((left, space, right)):
        copies["vis%d" % index] = local(
            vis_hbm.at[:, pl.ds(pl.multiple_of(block * T, T), T)], vis.at[index], 6 + index
        )
    early = ("tok", "cot", "vis0", "vis1", "vis2", "tau_space", "tau_band", "wqs")
    late = ("wob", "wos", "wqb")
    for name in early:
        copies[name].start()

    barrier = pltpu.get_barrier_semaphore()
    for other in (left, right):
        pl.semaphore_signal(barrier, inc=1, device_id=(band, other), device_id_type=MESH)
    for step in range(1, bands):
        pl.semaphore_signal(
            barrier,
            inc=1,
            device_id=(lax.rem(band + step, bands), space),
            device_id_type=MESH,
        )
    pl.semaphore_wait(barrier, bands + 1)

    def neighbours(source, target, index):
        return [
            pltpu.make_async_remote_copy(
                src_ref=source.at[pl.ds(at, RADIUS)],
                dst_ref=target.at[pl.ds(at, RADIUS)],
                send_sem=near_send.at[index, side],
                recv_sem=near_recv.at[index, side],
                device_id=(band, other),
                device_id_type=MESH,
            )
            for side, at, other in ((0, RADIUS, right), (1, 0, left))
        ]

    near = [
        neighbours(tok_hbm.at[0], halo, 0),
        neighbours(attended, attended_rim, 1),
        neighbours(stats, stats_rim, 2),
    ]
    for copy in near[0]:
        copy.start()

    def exchange(phase, step):
        other = lax.rem(band + step, bands)
        return pltpu.make_async_remote_copy(
            src_ref=sent.at[phase, other],
            dst_ref=got.at[phase, band],
            send_sem=all_send.at[phase, step],
            recv_sem=all_recv.at[phase, step],
            device_id=(other, space),
            device_id_type=MESH,
        )

    def scatter(phase, rows):
        pieces = [
            rows[:, :HALF].reshape(bands, count, HALF),
            rows[:, HALF:].reshape(bands, count, HALF),
        ]
        sent[phase] = jnp.concatenate(pieces, axis=1).astype(BF16)
        for step in range(1, bands):
            exchange(phase, step).start()
        got[phase, band] = sent[phase, band]

    def unpacked(slots):
        rows = slots.astype(F32)
        return jnp.concatenate(
            [rows[:, :count].reshape(T, HALF), rows[:, count:].reshape(T, HALF)], axis=1
        )

    def collect(phase):
        for step in range(1, bands):
            exchange(phase, step).wait_recv()
        return unpacked(got[phase])

    toward = lax.rem(space + spaces - 1 + 2 * lax.div(band, bands // 2), spaces)

    def far(step):
        other = lax.rem(band + step, bands)
        return pltpu.make_async_remote_copy(
            src_ref=sent.at[3, other],
            dst_ref=got_rim.at[band],
            send_sem=far_send.at[step],
            recv_sem=far_recv.at[band],
            device_id=(other, toward),
            device_id_type=MESH,
        )

    def far_arrival(sender):
        return pltpu.make_async_remote_copy(
            src_ref=sent.at[3, sender],
            dst_ref=got_rim.at[sender],
            send_sem=far_send.at[sender],
            recv_sem=far_recv.at[sender],
            device_id=(band, toward),
            device_id_type=MESH,
        )

    low = lax.broadcasted_iota(jnp.int32, (T, 128), 1) < HEAD_DIM
    ones = jnp.where(
        (lax.broadcasted_iota(jnp.int32, (256, 256), 0) >> 6)
        == (lax.broadcasted_iota(jnp.int32, (256, 256), 1) >> 6),
        1.0,
        0.0,
    ).astype(BF16)
    for pair in range(PAIRS):
        values[pair, :, 128:] = jnp.ones((2 * T, 128), BF16)
        values_two[pair, :, 128:] = jnp.ones((T, 128), BF16)

    copies["cot"].wait()
    scatter(0, cot[...].astype(F32))

    for index in range(3):
        copies["vis%d" % index].wait()
    group = lax.broadcasted_iota(jnp.int32, (bands, 128), 0)
    lane = lax.broadcasted_iota(jnp.int32, (bands, 128), 1)

    def own_row(index):
        return jnp.sum(jnp.where(group == band, vis[index], 0), axis=0, keepdims=True)

    row = lax.broadcasted_iota(jnp.int32, (T, T), 0)
    col = lax.broadcasted_iota(jnp.int32, (T, T), 1)
    own_seen = own_row(1) == 1
    rim_seen = jnp.where(lane[:1] < RADIUS, own_row(2), own_row(0)) == 1

    def within(offset):
        return (offset >= -RADIUS) & (offset <= RADIUS)

    def flag(test):
        return jnp.where(test, 1.0, 0.0)

    mask_own = flag(within(row - col) & (own_seen | (row == col)))
    mask_rim = flag(within(jnp.where(col < RADIUS, col + T, col - T) - row) & rim_seen)
    mask_back = flag(within(jnp.where(row < RADIUS, row + T, row - T) - col) & own_seen)
    pick = flag(row == band * count + lax.rem(col, count))
    spread = dot(vis[1].astype(F32), pick)
    seen = jnp.sum(
        jnp.where(group == lax.div(lane, count), spread, 0.0), axis=0, keepdims=True
    )
    same = lax.rem(row, count) == lax.rem(col, count)
    mask_two = flag(same & ((seen > 0.5) | (row == col)))

    copies["tau_space"].wait()
    copies["tau_band"].wait()

    def scale_row(tau):
        pieces = [
            jnp.where(low[:1], tau[2 * pair], tau[2 * pair + 1]) * (1.0 / HEAD_DIM)
            for pair in range(PAIRS)
        ]
        return jnp.concatenate(pieces, axis=1)

    scale_space = scale_row(tau_space)
    scale_band = scale_row(tau_band)

    def put_queries(slot, unit, scale):
        scaled = unit * scale
        for pair in range(PAIRS):
            queries[slot, pair] = stacked(scaled[:, lanes(pair)], low)

    def normed_heads(normed, weight, slot, which):
        raw = dot(normed, weight)
        factor = head_factor(raw, ones)
        unit = raw * factor
        if which is not None:
            which[0][slot] = unit
            which[1][slot] = factor
        return unit

    copies["tok"].wait()
    inputs = tok[...].astype(F32)
    normed = (inputs * row_factor(inputs)).astype(BF16)
    copies["wqs"].wait()
    for name in late:
        copies[name].start()
    put_queries(0, normed_heads(normed, wqs[:, :D], 0, (unit_q, fact_q)), scale_space)
    keys[:T] = normed_heads(normed, wqs[:, D : 2 * D], 0, (unit_k, fact_k)).astype(BF16)
    raw = dot(normed, wqs[:, 2 * D :]).astype(BF16)
    for pair in range(PAIRS):
        values[pair, :T, :128] = raw[:, lanes(pair)]
    for pair in range(PAIRS):
        weight = grown(queries[0, pair], keys[:T, lanes(pair)], mask_own)
        grown_one[pair, :, :T] = weight
        partial[pair] = dot(weight, values[pair, :T])

    for copy in near[0]:
        copy.wait_recv()
    rim = halo[...].astype(F32)
    normed = (rim * row_factor(rim)).astype(BF16)
    keys[T:] = normed_heads(normed, wqs[:, D : 2 * D], None, None).astype(BF16)
    raw = dot(normed, wqs[:, 2 * D :]).astype(BF16)
    for pair in range(PAIRS):
        values[pair, T:, :128] = raw[:, lanes(pair)]
    table = jnp.zeros((T, 128), F32)
    for pair in range(PAIRS):
        weight = grown(queries[0, pair], keys[T:, lanes(pair)], mask_rim)
        grown_one[pair, :, T:] = weight
        out = partial[pair] + dot(weight, values[pair, T:])
        turned = 1.0 / out[:, 128:]
        inverse[0, pair] = turned
        attended[:, lanes(pair)] = paired(low, out[:, :128] * turned).astype(BF16)
        table = jnp.where(col == 2 * pair, turned[:T], table)
        table = jnp.where(col == 2 * pair + 1, turned[T:], table)
    stats[...] = table
    copies["wos"].wait()
    after[...] = (inputs + dot(attended[...], wos[...])).astype(BF16)
    scatter(1, after[...].astype(F32))
    for index in (1, 2):
        for copy in near[index]:
            copy.start()

    upstream = collect(0)
    copies["wob"].wait()
    grad_att = dot_nt(upstream.astype(BF16), wob[...])
    for pair in range(PAIRS):
        ups_stack[pair] = stacked(grad_att[:, lanes(pair)], low)
    put_queries(2, normed_heads(normed, wqs[:, :D], None, None), scale_space)
    copies["wqb"].wait()
    for at in range(0, 3 * D, 256):
        wqb_t[at : at + 256] = wqb[:, at : at + 256].T

    rows = collect(1)
    fact_two = row_factor(rows)
    unit_two = rows * fact_two
    normed = unit_two.astype(BF16)
    put_queries(1, normed_heads(normed, wqb[:, :D], 1, (unit_q, fact_q)), scale_band)
    keys_two[...] = normed_heads(normed, wqb[:, D : 2 * D], 1, (unit_k, fact_k)).astype(BF16)
    raw = dot(normed, wqb[:, 2 * D :]).astype(BF16)
    for pair in range(PAIRS):
        values_two[pair, :, :128] = raw[:, lanes(pair)]
    outs = []
    for pair in range(PAIRS):
        at = lanes(pair)
        query, key, value, ups = queries[1, pair], keys_two[:, at], values_two[pair], ups_stack[pair]
        weight = grown(query, key, mask_two)
        out = dot(weight, value)
        turned = 1.0 / out[:, 128:]
        out = out[:, :128] * turned
        outs.append(paired(low, out))
        ups_f = ups.astype(F32)
        dscore = inner(ups, (-ups_f * out).astype(BF16), value) * turned
        dscore = (weight.astype(F32) * dscore).astype(BF16)
        grads[:, at] = paired(low, dot(dscore, key)) * scale_band[:, at]
        grads[:, D + pair * 128 : D + pair * 128 + 128] = dot_tn(dscore, query)
        wide[:, 2 * D + pair * 128 : 2 * D + pair * 128 + 128] = dot_tn(
            weight, (ups_f * turned).astype(BF16)
        ).astype(BF16)
    wide[:, :D] = head_back(unit_q[1], fact_q[1], grads[:, :D], ones).astype(BF16)
    wide[:, D : 2 * D] = head_back(unit_k[1], fact_k[1], grads[:, D:], ones).astype(BF16)
    back = dot(wide[...], wqb_t[...])
    scatter(3, upstream + row_back(unit_two, fact_two, back))
    for step in range(bands):
        far(step).start()
    scatter(2, jnp.concatenate(outs, axis=1))

    for at in range(0, 3 * D, 256):
        wqs_t[at : at + 256] = wqs[:, at : at + 256].T
    for at in range(0, D, 256):
        wos_t[at : at + 256] = wos[:, at : at + 256].T
    for index in (1, 2):
        for copy in near[index]:
            copy.wait_recv()
    for pair in range(PAIRS):
        grown_rim[pair] = grown(queries[2, pair], keys[:T, lanes(pair)], mask_back)
        for part in range(2):
            head = 2 * pair + part
            inverse_rim[pair, part * T : part * T + T] = jnp.broadcast_to(
                stats_rim[:, head : head + 1], (T, 128)
            )

    grad_after = collect(3)
    grad_att = dot(grad_after.astype(BF16), wos_t[...])
    for pair in range(PAIRS):
        at = lanes(pair)
        query, value, weight = queries[0, pair], values[pair], grown_one[pair]
        ups_f = jnp.concatenate(
            [jnp.where(low, grad_att[:, at], 0.0), jnp.where(low, 0.0, grad_att[:, at])], axis=0
        )
        out = attended[:, at].astype(F32)
        turned = inverse[0, pair]
        dscore = inner(
            ups_f.astype(BF16),
            (-ups_f * jnp.concatenate([out, out], axis=0)).astype(BF16),
            value,
        )
        dscore = dscore * jnp.concatenate([turned, turned], axis=1)
        dscore = (weight.astype(F32) * dscore).astype(BF16)
        grads[:, at] = paired(low, dot(dscore, keys[:, at])) * scale_space[:, at]
        partial[pair, :T, :128] = dot_tn(dscore[:, :T], query)
        partial[pair, :T, 128:] = dot_tn(weight[:, :T], (ups_f * turned).astype(BF16))
    wide[:, :D] = head_back(unit_q[0], fact_q[0], grads[:, :D], ones).astype(BF16)
    back = dot(wide[:, :D], wqs_t[:D])
    mixed[...] = after[...].astype(F32) + dot(collect(2).astype(BF16), wob[...])
    copies["mixed"].start()

    for sender in range(bands):
        far_arrival(sender).wait_recv()
    grad_att = dot(unpacked(got_rim[...]).astype(BF16), wos_t[...])
    for pair in range(PAIRS):
        at = lanes(pair)
        query, weight, turned = queries[2, pair], grown_rim[pair], inverse_rim[pair]
        ups_f = jnp.concatenate(
            [jnp.where(low, grad_att[:, at], 0.0), jnp.where(low, 0.0, grad_att[:, at])], axis=0
        )
        out = attended_rim[:, at].astype(F32)
        dscore = inner(
            ups_f.astype(BF16),
            (-ups_f * jnp.concatenate([out, out], axis=0)).astype(BF16),
            values[pair, :T],
        )
        dscore = (weight.astype(F32) * (dscore * turned)).astype(BF16)
        grads[:, D + pair * 128 : D + pair * 128 + 128] = partial[pair, :T, :128] + dot_tn(
            dscore, query
        )
        wide[:, 2 * D + pair * 128 : 2 * D + pair * 128 + 128] = (
            partial[pair, :T, 128:] + dot_tn(weight, (ups_f * turned).astype(BF16))
        ).astype(BF16)
    wide[:, D : 2 * D] = head_back(unit_k[0], fact_k[0], grads[:, D:], ones).astype(BF16)
    back = back + dot(wide[:, D:], wqs_t[D:])
    inputs = tok[...].astype(F32)
    fact_one = row_factor(inputs)
    grad[...] = grad_after + row_back(inputs * fact_one, fact_one, back)
    copies["grad"].start()

    for index in range(3):
        for copy in near[index]:
            copy.wait_send()
    for phase in range(4):
        for step in range(1, bands):
            exchange(phase, step).wait_send()
    for step in range(bands):
        far(step).wait_send()
    copies["mixed"].wait()
    copies["grad"].wait()


def per_device(bands, spaces, *arrays):
    hbm = pl.BlockSpec(memory_space=pltpu.HBM)
    out = jax.ShapeDtypeStruct((1, T, D), F32)
    count = T // bands
    dma = pltpu.SemaphoreType.DMA
    scratch = [
        pltpu.VMEM((T, D), BF16),
        pltpu.VMEM((T, D), BF16),
        pltpu.VMEM((T, D), BF16),
        pltpu.VMEM((3, bands, T), jnp.int32),
        pltpu.SMEM((HEADS,), F32),
        pltpu.SMEM((HEADS,), F32),
        pltpu.VMEM((D, 3 * D), BF16),
        pltpu.VMEM((D, D), BF16),
        pltpu.VMEM((D, 3 * D), BF16),
        pltpu.VMEM((D, D), BF16),
        pltpu.VMEM((3 * D, D), BF16),
        pltpu.VMEM((D, D), BF16),
        pltpu.VMEM((3 * D, D), BF16),
        pltpu.VMEM((2 * T, D), BF16),
        pltpu.VMEM((PAIRS, 2 * T, 256), BF16),
        pltpu.VMEM((T, D), BF16),
        pltpu.VMEM((PAIRS, T, 256), BF16),
        pltpu.VMEM((3, PAIRS, 2 * T, 128), BF16),
        pltpu.VMEM((PAIRS, 2 * T, 128), BF16),
        pltpu.VMEM((PAIRS, 2 * T, 2 * T), BF16),
        pltpu.VMEM((PAIRS, 2 * T, T), BF16),
        pltpu.VMEM((PAIRS, 2 * T, 256), F32),
        pltpu.VMEM((1, PAIRS, 2 * T, 128), F32),
        pltpu.VMEM((PAIRS, 2 * T, 128), F32),
        pltpu.VMEM((2, T, D), F32),
        pltpu.VMEM((2, T, D), F32),
        pltpu.VMEM((2, T, D), F32),
        pltpu.VMEM((2, T, D), F32),
        pltpu.VMEM((T, 3 * D), BF16),
        pltpu.VMEM((T, D), BF16),
        pltpu.VMEM((T, D), BF16),
        pltpu.VMEM((T, D), BF16),
        pltpu.VMEM((T, 128), F32),
        pltpu.VMEM((T, 128), F32),
        pltpu.VMEM((T, 2 * D), F32),
        pltpu.VMEM((4, bands, 2 * count, HALF), BF16),
        pltpu.VMEM((4, bands, 2 * count, HALF), BF16),
        pltpu.VMEM((bands, 2 * count, HALF), BF16),
        pltpu.VMEM((T, D), F32),
        pltpu.VMEM((T, D), F32),
        dma((13,)),
        dma((3, 2)),
        dma((3, 2)),
        dma((4, bands)),
        dma((4, bands)),
        dma((bands,)),
        dma((bands,)),
    ]
    return pl.pallas_call(
        functools.partial(kernel, bands, spaces),
        out_shape=(out, out),
        in_specs=[hbm] * 9,
        out_specs=(hbm, hbm),
        scratch_shapes=scratch,
        compiler_params=pltpu.CompilerParams(
            collective_id=0, has_side_effects=True, vmem_limit_bytes=64 * 1024 * 1024 - 65536
        ),
        cost_estimate=pl.CostEstimate(
            flops=3_500_000_000, bytes_accessed=11_000_000, transcendentals=600_000
        ),
    )(*arrays)


def solution(mesh):
    cells = P("band", "space", None)
    return jax.shard_map(
        functools.partial(per_device, mesh.shape["band"], mesh.shape["space"]),
        mesh=mesh,
        in_specs=(cells, cells, P(), P(), P(), P(), P(), P(), P()),
        out_specs=(cells, cells),
        check_vma=False,
    )
```

```python
import functools

import jax
import jax.numpy as jnp
from jax import lax
from jax.experimental import pallas as pl
from jax.experimental.pallas import tpu as pltpu
from jax.sharding import PartitionSpec as P

D = 768
HALF = D // 2
HEADS = 12
HEAD_DIM = 64
PAIRS = HEADS // 2
T = 128
RADIUS = 64
EPS = 1e-06
MESH = pl.DeviceIdType.MESH
F32 = jnp.float32
BF16 = jnp.bfloat16


def dot(left, right):
    return jnp.dot(left, right, preferred_element_type=F32)


def dot_nt(left, right):
    return lax.dot_general(left, right, (((1,), (1,)), ((), ())), preferred_element_type=F32)


def dot_tn(left, right):
    return lax.dot_general(left, right, (((0,), (0,)), ((), ())), preferred_element_type=F32)


def row_factor(values):
    return lax.rsqrt(jnp.sum(values * values, axis=-1, keepdims=True) * (1.0 / D) + EPS)


def row_back(unit, factor, upstream):
    return factor * (upstream - unit * (jnp.sum(unit * upstream, axis=-1, keepdims=True) * (1.0 / D)))


def head_means(values, ones):
    low = values.astype(BF16)
    width = ones.shape[0]
    parts = [dot(low[:, at : at + width], ones) for at in range(0, values.shape[1], width)]
    return jnp.concatenate(parts, axis=1) * (1.0 / HEAD_DIM)


def head_factor(values, ones):
    return lax.rsqrt(head_means(values * values, ones) + EPS)


def head_back(unit, factor, upstream, ones):
    return factor * (upstream - unit * head_means(unit * upstream, ones))


def stacked(pair, low):
    return jnp.concatenate([jnp.where(low, pair, 0.0), jnp.where(low, 0.0, pair)], axis=0).astype(BF16)


def lanes(pair):
    return slice(pair * 128, pair * 128 + 128)


def paired(low, stack):
    return jnp.where(low, stack[:T], stack[T:])


def grown(query_stack, keys, mask):
    scores = jnp.exp(dot_nt(query_stack, keys))
    return jnp.concatenate([scores[:T] * mask, scores[T:] * mask], axis=0).astype(BF16)


def inner(ups, outs, values_one):
    return dot_nt(jnp.concatenate([ups, outs], axis=1), values_one)


def kernel(
    bands,
    spaces,
    tok_hbm,
    cot_hbm,
    vis_hbm,
    tau_space_hbm,
    tau_band_hbm,
    wqs_hbm,
    wos_hbm,
    wqb_hbm,
    wob_hbm,
    mixed,
    grad,
    tok,
    halo,
    cot,
    vis,
    tau_space,
    tau_band,
    wqs,
    wos,
    wqb,
    wob,
    wqs_t,
    wos_t,
    wqb_t,
    keys,
    values,
    keys_two,
    values_two,
    queries,
    ups_stack,
    grown_one,
    grown_rim,
    partial,
    inverse,
    inverse_rim,
    unit_q,
    fact_q,
    unit_k,
    fact_k,
    wide,
    after,
    attended,
    attended_rim,
    stats,
    stats_rim,
    grads,
    sent,
    got,
    got_rim,
    local_sem,
    near_send,
    near_recv,
    all_send,
    all_recv,
    far_send,
    far_recv,
):
    band = lax.axis_index("band")
    space = lax.axis_index("space")
    count = T // bands
    right = lax.rem(space + 1, spaces)
    left = lax.rem(space + spaces - 1, spaces)

    def local(source, target, index):
        return pltpu.make_async_copy(source, target, local_sem.at[index])

    copies = {
        "tok": local(tok_hbm.at[0], tok, 0),
        "wqs": local(wqs_hbm, wqs, 1),
        "cot": local(cot_hbm.at[0], cot, 2),
        "wos": local(wos_hbm, wos, 3),
        "wob": local(wob_hbm, wob, 4),
        "wqb": local(wqb_hbm, wqb, 5),
        "tau_space": local(tau_space_hbm, tau_space, 9),
        "tau_band": local(tau_band_hbm, tau_band, 10),
    }
    for index, block in enumerate((left, space, right)):
        copies["vis%d" % index] = local(
            vis_hbm.at[:, pl.ds(pl.multiple_of(block * T, T), T)], vis.at[index], 6 + index
        )
    early = ("tok", "cot", "vis0", "vis1", "vis2", "tau_space", "tau_band", "wqs")
    late = ("wob", "wos", "wqb")
    for name in early:
        copies[name].start()

    barrier = pltpu.get_barrier_semaphore()
    for other in (left, right):
        pl.semaphore_signal(barrier, inc=1, device_id=(band, other), device_id_type=MESH)
    for step in range(1, bands):
        pl.semaphore_signal(
            barrier,
            inc=1,
            device_id=(lax.rem(band + step, bands), space),
            device_id_type=MESH,
        )
    pl.semaphore_wait(barrier, bands + 1)

    def neighbours(source, target, index):
        return [
            pltpu.make_async_remote_copy(
                src_ref=source.at[pl.ds(at, RADIUS)],
                dst_ref=target.at[pl.ds(at, RADIUS)],
                send_sem=near_send.at[index, side],
                recv_sem=near_recv.at[index, side],
                device_id=(band, other),
                device_id_type=MESH,
            )
            for side, at, other in ((0, RADIUS, right), (1, 0, left))
        ]

    near = [
        neighbours(tok_hbm.at[0], halo, 0),
        neighbours(attended, attended_rim, 1),
        neighbours(stats, stats_rim, 2),
    ]
    for copy in near[0]:
        copy.start()

    def exchange(phase, step):
        other = lax.rem(band + step, bands)
        return pltpu.make_async_remote_copy(
            src_ref=sent.at[phase, other],
            dst_ref=got.at[phase, band],
            send_sem=all_send.at[phase, step],
            recv_sem=all_recv.at[phase, step],
            device_id=(other, space),
            device_id_type=MESH,
        )

    def scatter(phase, rows):
        pieces = [
            rows[:, :HALF].reshape(bands, count, HALF),
            rows[:, HALF:].reshape(bands, count, HALF),
        ]
        sent[phase] = jnp.concatenate(pieces, axis=1).astype(BF16)
        for step in range(1, bands):
            exchange(phase, step).start()
        got[phase, band] = sent[phase, band]

    def unpacked(slots):
        rows = slots.astype(F32)
        return jnp.concatenate(
            [rows[:, :count].reshape(T, HALF), rows[:, count:].reshape(T, HALF)], axis=1
        )

    def collect(phase):
        for step in range(1, bands):
            exchange(phase, step).wait_recv()
        return unpacked(got[phase])

    toward = lax.rem(space + spaces - 1 + 2 * lax.div(band, bands // 2), spaces)

    def far(step):
        other = lax.rem(band + step, bands)
        return pltpu.make_async_remote_copy(
            src_ref=sent.at[3, other],
            dst_ref=got_rim.at[band],
            send_sem=far_send.at[step],
            recv_sem=far_recv.at[band],
            device_id=(other, toward),
            device_id_type=MESH,
        )

    def far_arrival(sender):
        return pltpu.make_async_remote_copy(
            src_ref=sent.at[3, sender],
            dst_ref=got_rim.at[sender],
            send_sem=far_send.at[sender],
            recv_sem=far_recv.at[sender],
            device_id=(band, toward),
            device_id_type=MESH,
        )

    low = lax.broadcasted_iota(jnp.int32, (T, 128), 1) < HEAD_DIM
    ones = jnp.where(
        (lax.broadcasted_iota(jnp.int32, (256, 256), 0) >> 6)
        == (lax.broadcasted_iota(jnp.int32, (256, 256), 1) >> 6),
        1.0,
        0.0,
    ).astype(BF16)
    for pair in range(PAIRS):
        values[pair, :, 128:] = jnp.ones((2 * T, 128), BF16)
        values_two[pair, :, 128:] = jnp.ones((T, 128), BF16)

    copies["cot"].wait()
    scatter(0, cot[...].astype(F32))

    for index in range(3):
        copies["vis%d" % index].wait()
    group = lax.broadcasted_iota(jnp.int32, (bands, 128), 0)
    lane = lax.broadcasted_iota(jnp.int32, (bands, 128), 1)

    def own_row(index):
        return jnp.sum(jnp.where(group == band, vis[index], 0), axis=0, keepdims=True)

    row = lax.broadcasted_iota(jnp.int32, (T, T), 0)
    col = lax.broadcasted_iota(jnp.int32, (T, T), 1)
    own_seen = own_row(1) == 1
    rim_seen = jnp.where(lane[:1] < RADIUS, own_row(2), own_row(0)) == 1

    def within(offset):
        return (offset >= -RADIUS) & (offset <= RADIUS)

    def flag(test):
        return jnp.where(test, 1.0, 0.0)

    mask_own = flag(within(row - col) & (own_seen | (row == col)))
    mask_rim = flag(within(jnp.where(col < RADIUS, col + T, col - T) - row) & rim_seen)
    mask_back = flag(within(jnp.where(row < RADIUS, row + T, row - T) - col) & own_seen)
    pick = flag(row == band * count + lax.rem(col, count))
    spread = dot(vis[1].astype(F32), pick)
    seen = jnp.sum(
        jnp.where(group == lax.div(lane, count), spread, 0.0), axis=0, keepdims=True
    )
    same = lax.rem(row, count) == lax.rem(col, count)
    mask_two = flag(same & ((seen > 0.5) | (row == col)))

    copies["tau_space"].wait()
    copies["tau_band"].wait()

    def scale_row(tau):
        pieces = [
            jnp.where(low[:1], tau[2 * pair], tau[2 * pair + 1]) * (1.0 / HEAD_DIM)
            for pair in range(PAIRS)
        ]
        return jnp.concatenate(pieces, axis=1)

    scale_space = scale_row(tau_space)
    scale_band = scale_row(tau_band)

    def put_queries(slot, unit, scale):
        scaled = unit * scale
        for pair in range(PAIRS):
            queries[slot, pair] = stacked(scaled[:, lanes(pair)], low)

    def normed_heads(normed, weight, slot, which):
        raw = dot(normed, weight)
        factor = head_factor(raw, ones)
        unit = raw * factor
        if which is not None:
            which[0][slot] = unit
            which[1][slot] = factor
        return unit

    copies["tok"].wait()
    inputs = tok[...].astype(F32)
    normed = (inputs * row_factor(inputs)).astype(BF16)
    copies["wqs"].wait()
    for name in late:
        copies[name].start()
    put_queries(0, normed_heads(normed, wqs[:, :D], 0, (unit_q, fact_q)), scale_space)
    keys[:T] = normed_heads(normed, wqs[:, D : 2 * D], 0, (unit_k, fact_k)).astype(BF16)
    raw = dot(normed, wqs[:, 2 * D :]).astype(BF16)
    for pair in range(PAIRS):
        values[pair, :T, :128] = raw[:, lanes(pair)]
    for pair in range(PAIRS):
        grown_one[pair, :, :T] = grown(queries[0, pair], keys[:T, lanes(pair)], mask_own)
    for pair in range(PAIRS):
        partial[pair] = dot(grown_one[pair, :, :T], values[pair, :T])

    for copy in near[0]:
        copy.wait_recv()
    rim = halo[...].astype(F32)
    normed = (rim * row_factor(rim)).astype(BF16)
    keys[T:] = normed_heads(normed, wqs[:, D : 2 * D], None, None).astype(BF16)
    raw = dot(normed, wqs[:, 2 * D :]).astype(BF16)
    for pair in range(PAIRS):
        values[pair, T:, :128] = raw[:, lanes(pair)]
    for pair in range(PAIRS):
        grown_one[pair, :, T:] = grown(queries[0, pair], keys[T:, lanes(pair)], mask_rim)
    for pair in range(PAIRS):
        out = partial[pair] + dot(grown_one[pair, :, T:], values[pair, T:])
        turned = 1.0 / out[:, 128:]
        inverse[0, pair] = turned
        attended[:, lanes(pair)] = paired(low, out[:, :128] * turned).astype(BF16)
    copies["wos"].wait()
    after[...] = (inputs + dot(attended[...], wos[...])).astype(BF16)
    scatter(1, after[...].astype(F32))
    table = jnp.zeros((T, 128), F32)
    for pair in range(PAIRS):
        table = jnp.where(col == 2 * pair, inverse[0, pair, :T], table)
        table = jnp.where(col == 2 * pair + 1, inverse[0, pair, T:], table)
    stats[...] = table
    for index in (1, 2):
        for copy in near[index]:
            copy.start()

    upstream = collect(0)
    copies["wob"].wait()
    grad_att = dot_nt(upstream.astype(BF16), wob[...])
    for pair in range(PAIRS):
        ups_stack[pair] = stacked(grad_att[:, lanes(pair)], low)
    put_queries(2, normed_heads(normed, wqs[:, :D], None, None), scale_space)
    copies["wqb"].wait()
    for at in range(0, 3 * D, 256):
        wqb_t[at : at + 256] = wqb[:, at : at + 256].T

    rows = collect(1)
    fact_two = row_factor(rows)
    unit_two = rows * fact_two
    normed = unit_two.astype(BF16)
    put_queries(1, normed_heads(normed, wqb[:, :D], 1, (unit_q, fact_q)), scale_band)
    keys_two[...] = normed_heads(normed, wqb[:, D : 2 * D], 1, (unit_k, fact_k)).astype(BF16)
    raw = dot(normed, wqb[:, 2 * D :]).astype(BF16)
    for pair in range(PAIRS):
        values_two[pair, :, :128] = raw[:, lanes(pair)]
    everyone = range(PAIRS)
    weight = [grown(queries[1, p], keys_two[:, lanes(p)], mask_two) for p in everyone]
    outs, turned = [], []
    for pair in everyone:
        out = dot(weight[pair], values_two[pair])
        turned.append(1.0 / out[:, 128:])
        outs.append(out[:, :128] * turned[pair])
    dscore = []
    for pair in everyone:
        ups = ups_stack[pair]
        inside = inner(ups, (-ups.astype(F32) * outs[pair]).astype(BF16), values_two[pair])
        dscore.append((weight[pair].astype(F32) * (inside * turned[pair])).astype(BF16))
    for pair in everyone:
        at = lanes(pair)
        grads[:, at] = paired(low, dot(dscore[pair], keys_two[:, at])) * scale_band[:, at]
        grads[:, D + pair * 128 : D + pair * 128 + 128] = dot_tn(dscore[pair], queries[1, pair])
        wide[:, 2 * D + pair * 128 : 2 * D + pair * 128 + 128] = dot_tn(
            weight[pair], (ups_stack[pair].astype(F32) * turned[pair]).astype(BF16)
        ).astype(BF16)
    outs = [paired(low, out) for out in outs]
    wide[:, :D] = head_back(unit_q[1], fact_q[1], grads[:, :D], ones).astype(BF16)
    wide[:, D : 2 * D] = head_back(unit_k[1], fact_k[1], grads[:, D:], ones).astype(BF16)
    back = dot(wide[...], wqb_t[...])
    scatter(3, upstream + row_back(unit_two, fact_two, back))
    for step in range(bands):
        far(step).start()
    scatter(2, jnp.concatenate(outs, axis=1))

    for at in range(0, 3 * D, 256):
        wqs_t[at : at + 256] = wqs[:, at : at + 256].T
    for at in range(0, D, 256):
        wos_t[at : at + 256] = wos[:, at : at + 256].T
    for index in (1, 2):
        for copy in near[index]:
            copy.wait_recv()
    for pair in range(PAIRS):
        grown_rim[pair] = grown(queries[2, pair], keys[:T, lanes(pair)], mask_back)
        for part in range(2):
            head = 2 * pair + part
            inverse_rim[pair, part * T : part * T + T] = jnp.broadcast_to(
                stats_rim[:, head : head + 1], (T, 128)
            )

    grad_after = collect(3)
    grad_att = dot(grad_after.astype(BF16), wos_t[...])
    def stacked_ups():
        return [
            jnp.concatenate(
                [jnp.where(low, part, 0.0), jnp.where(low, 0.0, part)], axis=0
            )
            for part in (grad_att[:, lanes(pair)] for pair in range(PAIRS))
        ]

    def window_dscore(ups, weight, outs, value, turned):
        out = jnp.concatenate([outs, outs], axis=0).astype(F32)
        inside = inner(ups.astype(BF16), (-ups * out).astype(BF16), value)
        return (weight.astype(F32) * (inside * turned)).astype(BF16)

    ups_all = stacked_ups()
    dscore = []
    for pair in range(PAIRS):
        turned = inverse[0, pair]
        turned = jnp.concatenate([turned, turned], axis=1)
        dscore.append(
            window_dscore(
                ups_all[pair], grown_one[pair], attended[:, lanes(pair)], values[pair], turned
            )
        )
    for pair in range(PAIRS):
        at = lanes(pair)
        grads[:, at] = paired(low, dot(dscore[pair], keys[:, at])) * scale_space[:, at]
        partial[pair, :T, :128] = dot_tn(dscore[pair][:, :T], queries[0, pair])
        partial[pair, :T, 128:] = dot_tn(
            grown_one[pair, :, :T], (ups_all[pair] * inverse[0, pair]).astype(BF16)
        )
    wide[:, :D] = head_back(unit_q[0], fact_q[0], grads[:, :D], ones).astype(BF16)
    back = dot(wide[:, :D], wqs_t[:D])
    mixed[0] = after[...].astype(F32) + dot(collect(2).astype(BF16), wob[...])

    for sender in range(bands):
        far_arrival(sender).wait_recv()
    grad_att = dot(unpacked(got_rim[...]).astype(BF16), wos_t[...])
    ups_all = stacked_ups()
    dscore = [
        window_dscore(
            ups_all[pair],
            grown_rim[pair],
            attended_rim[:, lanes(pair)],
            values[pair, :T],
            inverse_rim[pair],
        )
        for pair in range(PAIRS)
    ]
    for pair in range(PAIRS):
        grads[:, D + pair * 128 : D + pair * 128 + 128] = partial[pair, :T, :128] + dot_tn(
            dscore[pair], queries[2, pair]
        )
        wide[:, 2 * D + pair * 128 : 2 * D + pair * 128 + 128] = (
            partial[pair, :T, 128:]
            + dot_tn(grown_rim[pair], (ups_all[pair] * inverse_rim[pair]).astype(BF16))
        ).astype(BF16)
    wide[:, D : 2 * D] = head_back(unit_k[0], fact_k[0], grads[:, D:], ones).astype(BF16)
    back = back + dot(wide[:, D:], wqs_t[D:])
    inputs = tok[...].astype(F32)
    fact_one = row_factor(inputs)
    grad[0] = grad_after + row_back(inputs * fact_one, fact_one, back)

    for index in range(3):
        for copy in near[index]:
            copy.wait_send()
    for phase in range(4):
        for step in range(1, bands):
            exchange(phase, step).wait_send()
    for step in range(bands):
        far(step).wait_send()


def deliver(mixed, grad, mixed_hbm, grad_hbm, sem):
    copies = [
        pltpu.make_async_copy(
            source.at[0, pl.ds(part * 32, 32)],
            target.at[0, pl.ds(part * 32, 32)],
            sem.at[which, part],
        )
        for part in range(4)
        for which, (source, target) in enumerate(((mixed, mixed_hbm), (grad, grad_hbm)))
    ]
    for copy in copies:
        copy.start()
    for copy in copies:
        copy.wait()


def per_device(bands, spaces, *arrays):
    kept = pltpu.VMEM((1, T, D), F32)
    vmem = pl.BlockSpec(memory_space=pltpu.VMEM)
    hbm = pl.BlockSpec(memory_space=pltpu.HBM)
    out = jax.ShapeDtypeStruct((1, T, D), F32)
    count = T // bands
    dma = pltpu.SemaphoreType.DMA
    scratch = [
        pltpu.VMEM((T, D), BF16),
        pltpu.VMEM((T, D), BF16),
        pltpu.VMEM((T, D), BF16),
        pltpu.VMEM((3, bands, T), jnp.int32),
        pltpu.SMEM((HEADS,), F32),
        pltpu.SMEM((HEADS,), F32),
        pltpu.VMEM((D, 3 * D), BF16),
        pltpu.VMEM((D, D), BF16),
        pltpu.VMEM((D, 3 * D), BF16),
        pltpu.VMEM((D, D), BF16),
        pltpu.VMEM((3 * D, D), BF16),
        pltpu.VMEM((D, D), BF16),
        pltpu.VMEM((3 * D, D), BF16),
        pltpu.VMEM((2 * T, D), BF16),
        pltpu.VMEM((PAIRS, 2 * T, 256), BF16),
        pltpu.VMEM((T, D), BF16),
        pltpu.VMEM((PAIRS, T, 256), BF16),
        pltpu.VMEM((3, PAIRS, 2 * T, 128), BF16),
        pltpu.VMEM((PAIRS, 2 * T, 128), BF16),
        pltpu.VMEM((PAIRS, 2 * T, 2 * T), BF16),
        pltpu.VMEM((PAIRS, 2 * T, T), BF16),
        pltpu.VMEM((PAIRS, 2 * T, 256), F32),
        pltpu.VMEM((1, PAIRS, 2 * T, 128), F32),
        pltpu.VMEM((PAIRS, 2 * T, 128), F32),
        pltpu.VMEM((2, T, D), F32),
        pltpu.VMEM((2, T, D), F32),
        pltpu.VMEM((2, T, D), F32),
        pltpu.VMEM((2, T, D), F32),
        pltpu.VMEM((T, 3 * D), BF16),
        pltpu.VMEM((T, D), BF16),
        pltpu.VMEM((T, D), BF16),
        pltpu.VMEM((T, D), BF16),
        pltpu.VMEM((T, 128), F32),
        pltpu.VMEM((T, 128), F32),
        pltpu.VMEM((T, 2 * D), F32),
        pltpu.VMEM((4, bands, 2 * count, HALF), BF16),
        pltpu.VMEM((4, bands, 2 * count, HALF), BF16),
        pltpu.VMEM((bands, 2 * count, HALF), BF16),
        dma((11,)),
        dma((3, 2)),
        dma((3, 2)),
        dma((4, bands)),
        dma((4, bands)),
        dma((bands,)),
        dma((bands,)),
    ]
    made = pl.pallas_call(
        functools.partial(kernel, bands, spaces),
        out_shape=(kept, kept),
        in_specs=[hbm] * 9,
        out_specs=(vmem, vmem),
        scratch_shapes=scratch,
        compiler_params=pltpu.CompilerParams(
            collective_id=0, has_side_effects=True, vmem_limit_bytes=63 * 1024 * 1024
        ),
        cost_estimate=pl.CostEstimate(
            flops=3_500_000_000, bytes_accessed=11_000_000, transcendentals=600_000
        ),
    )(*arrays)
    return pl.pallas_call(
        deliver,
        out_shape=(out, out),
        in_specs=[vmem] * 2,
        out_specs=(hbm, hbm),
        scratch_shapes=[dma((2, 4))],
    )(*[pltpu.with_memory_space_constraint(part, pltpu.VMEM) for part in made])


def solution(mesh):
    cells = P("band", "space", None)
    return jax.shard_map(
        functools.partial(per_device, mesh.shape["band"], mesh.shape["space"]),
        mesh=mesh,
        in_specs=(cells, cells, P(), P(), P(), P(), P(), P(), P()),
        out_specs=(cells, cells),
        check_vma=False,
    )
```

```python
import functools

import jax
import jax.numpy as jnp
from jax import lax
from jax.experimental import pallas as pl
from jax.experimental.pallas import tpu as pltpu
from jax.sharding import PartitionSpec as P

D = 768
HALF = D // 2
HEADS = 12
HEAD_DIM = 64
PAIRS = HEADS // 2
T = 128
RADIUS = 64
EPS = 1e-06
MESH = pl.DeviceIdType.MESH
F32 = jnp.float32
BF16 = jnp.bfloat16


def dot(left, right):
    return jnp.dot(left, right, preferred_element_type=F32)


def dot_nt(left, right):
    return lax.dot_general(left, right, (((1,), (1,)), ((), ())), preferred_element_type=F32)


def dot_tn(left, right):
    return lax.dot_general(left, right, (((0,), (0,)), ((), ())), preferred_element_type=F32)


def row_factor(values):
    return lax.rsqrt(jnp.sum(values * values, axis=-1, keepdims=True) * (1.0 / D) + EPS)


def row_back(unit, factor, upstream):
    return factor * (upstream - unit * (jnp.sum(unit * upstream, axis=-1, keepdims=True) * (1.0 / D)))


def head_means(values, ones):
    low = values.astype(BF16)
    width = ones.shape[0]
    parts = [dot(low[:, at : at + width], ones) for at in range(0, values.shape[1], width)]
    return jnp.concatenate(parts, axis=1) * (1.0 / HEAD_DIM)


def head_factor(values, ones):
    return lax.rsqrt(head_means(values * values, ones) + EPS)


def head_back(unit, factor, upstream, ones):
    return factor * (upstream - unit * head_means(unit * upstream, ones))


def stacked(pair, low):
    return jnp.concatenate([jnp.where(low, pair, 0.0), jnp.where(low, 0.0, pair)], axis=0).astype(BF16)


def lanes(pair):
    return slice(pair * 128, pair * 128 + 128)


def paired(low, stack):
    return jnp.where(low, stack[:T], stack[T:])


def grown(query_stack, keys, mask):
    scores = jnp.exp(dot_nt(query_stack, keys))
    return jnp.concatenate([scores[:T] * mask, scores[T:] * mask], axis=0).astype(BF16)


def inner(ups, outs, values_one):
    return dot_nt(jnp.concatenate([ups, outs], axis=1), values_one)


def kernel(
    bands,
    spaces,
    tok_hbm,
    cot_hbm,
    vis_hbm,
    tau_space_hbm,
    tau_band_hbm,
    wqs_hbm,
    wos_hbm,
    wqb_hbm,
    wob_hbm,
    mixed,
    grad,
    tok,
    halo,
    cot,
    vis,
    tau_space,
    tau_band,
    wqs,
    wos,
    wqb,
    wob,
    wqs_t,
    wos_t,
    wqb_t,
    keys,
    values,
    keys_two,
    values_two,
    queries,
    ups_stack,
    grown_one,
    grown_rim,
    partial,
    inverse,
    inverse_rim,
    unit_q,
    fact_q,
    unit_k,
    fact_k,
    wide,
    after,
    attended,
    attended_rim,
    stats,
    stats_rim,
    grads,
    sent,
    got,
    got_rim,
    local_sem,
    near_send,
    near_recv,
    all_send,
    all_recv,
    far_send,
    far_recv,
):
    band = lax.axis_index("band")
    space = lax.axis_index("space")
    count = T // bands
    right = lax.rem(space + 1, spaces)
    left = lax.rem(space + spaces - 1, spaces)

    def local(source, target, index):
        return pltpu.make_async_copy(source, target, local_sem.at[index])

    copies = {
        "tok": local(tok_hbm.at[0], tok, 0),
        "wqs": local(wqs_hbm, wqs, 1),
        "cot": local(cot_hbm.at[0], cot, 2),
        "wos": local(wos_hbm, wos, 3),
        "wob": local(wob_hbm, wob, 4),
        "wqb": local(wqb_hbm, wqb, 5),
        "tau_space": local(tau_space_hbm, tau_space, 9),
        "tau_band": local(tau_band_hbm, tau_band, 10),
    }
    for index, block in enumerate((left, space, right)):
        copies["vis%d" % index] = local(
            vis_hbm.at[:, pl.ds(pl.multiple_of(block * T, T), T)], vis.at[index], 6 + index
        )
    early = ("tok", "cot", "vis0", "vis1", "vis2", "tau_space", "tau_band", "wqs")
    late = ("wob", "wos", "wqb")
    for name in early:
        copies[name].start()

    barrier = pltpu.get_barrier_semaphore()
    for other in (left, right):
        pl.semaphore_signal(barrier, inc=1, device_id=(band, other), device_id_type=MESH)
    for step in range(1, bands):
        pl.semaphore_signal(
            barrier,
            inc=1,
            device_id=(lax.rem(band + step, bands), space),
            device_id_type=MESH,
        )
    pl.semaphore_wait(barrier, bands + 1)

    def neighbours(source, target, index):
        return [
            pltpu.make_async_remote_copy(
                src_ref=source.at[pl.ds(at, RADIUS)],
                dst_ref=target.at[pl.ds(at, RADIUS)],
                send_sem=near_send.at[index, side],
                recv_sem=near_recv.at[index, side],
                device_id=(band, other),
                device_id_type=MESH,
            )
            for side, at, other in ((0, RADIUS, right), (1, 0, left))
        ]

    near = [
        neighbours(tok_hbm.at[0], halo, 0),
        neighbours(attended, attended_rim, 1),
        neighbours(stats, stats_rim, 2),
    ]
    for copy in near[0]:
        copy.start()

    def exchange(phase, step):
        other = lax.rem(band + step, bands)
        return pltpu.make_async_remote_copy(
            src_ref=sent.at[phase, other],
            dst_ref=got.at[phase, band],
            send_sem=all_send.at[phase, step],
            recv_sem=all_recv.at[phase, step],
            device_id=(other, space),
            device_id_type=MESH,
        )

    def scatter(phase, rows):
        pieces = [
            rows[:, :HALF].reshape(bands, count, HALF),
            rows[:, HALF:].reshape(bands, count, HALF),
        ]
        sent[phase] = jnp.concatenate(pieces, axis=1).astype(BF16)
        for step in range(1, bands):
            exchange(phase, step).start()
        got[phase, band] = sent[phase, band]

    def unpacked(slots):
        rows = slots.astype(F32)
        return jnp.concatenate(
            [rows[:, :count].reshape(T, HALF), rows[:, count:].reshape(T, HALF)], axis=1
        )

    def collect(phase):
        for step in range(1, bands):
            exchange(phase, step).wait_recv()
        return unpacked(got[phase])

    toward = lax.rem(space + spaces - 1 + 2 * lax.div(band, bands // 2), spaces)

    def far(step):
        other = lax.rem(band + step, bands)
        return pltpu.make_async_remote_copy(
            src_ref=sent.at[3, other],
            dst_ref=got_rim.at[band],
            send_sem=far_send.at[step],
            recv_sem=far_recv.at[band],
            device_id=(other, toward),
            device_id_type=MESH,
        )

    def far_arrival(sender):
        return pltpu.make_async_remote_copy(
            src_ref=sent.at[3, sender],
            dst_ref=got_rim.at[sender],
            send_sem=far_send.at[sender],
            recv_sem=far_recv.at[sender],
            device_id=(band, toward),
            device_id_type=MESH,
        )

    low = lax.broadcasted_iota(jnp.int32, (T, 128), 1) < HEAD_DIM
    ones = jnp.where(
        (lax.broadcasted_iota(jnp.int32, (256, 256), 0) >> 6)
        == (lax.broadcasted_iota(jnp.int32, (256, 256), 1) >> 6),
        1.0,
        0.0,
    ).astype(BF16)
    for pair in range(PAIRS):
        values[pair, :, 128:] = jnp.ones((2 * T, 128), BF16)
        values_two[pair, :, 128:] = jnp.ones((T, 128), BF16)

    for index in range(3):
        copies["vis%d" % index].wait()
    group = lax.broadcasted_iota(jnp.int32, (bands, 128), 0)
    lane = lax.broadcasted_iota(jnp.int32, (bands, 128), 1)

    def own_row(index):
        return jnp.sum(jnp.where(group == band, vis[index], 0), axis=0, keepdims=True)

    row = lax.broadcasted_iota(jnp.int32, (T, T), 0)
    col = lax.broadcasted_iota(jnp.int32, (T, T), 1)
    own_seen = own_row(1) == 1
    rim_seen = jnp.where(lane[:1] < RADIUS, own_row(2), own_row(0)) == 1

    def within(offset):
        return (offset >= -RADIUS) & (offset <= RADIUS)

    def flag(test):
        return jnp.where(test, 1.0, 0.0)

    mask_own = flag(within(row - col) & (own_seen | (row == col)))
    mask_rim = flag(within(jnp.where(col < RADIUS, col + T, col - T) - row) & rim_seen)
    mask_back = flag(within(jnp.where(row < RADIUS, row + T, row - T) - col) & own_seen)
    pick = flag(row == band * count + lax.rem(col, count))
    spread = dot(vis[1].astype(F32), pick)
    seen = jnp.sum(
        jnp.where(group == lax.div(lane, count), spread, 0.0), axis=0, keepdims=True
    )
    same = lax.rem(row, count) == lax.rem(col, count)
    mask_two = flag(same & ((seen > 0.5) | (row == col)))

    copies["tau_space"].wait()
    copies["tau_band"].wait()

    def scale_row(tau):
        pieces = [
            jnp.where(low[:1], tau[2 * pair], tau[2 * pair + 1]) * (1.0 / HEAD_DIM)
            for pair in range(PAIRS)
        ]
        return jnp.concatenate(pieces, axis=1)

    scale_space = scale_row(tau_space)
    scale_band = scale_row(tau_band)

    def put_queries(slot, unit, scale):
        scaled = unit * scale
        for pair in range(PAIRS):
            queries[slot, pair] = stacked(scaled[:, lanes(pair)], low)

    def normed_heads(normed, weight, slot, which):
        raw = dot(normed, weight)
        factor = head_factor(raw, ones)
        unit = raw * factor
        if which is not None:
            which[0][slot] = unit
            which[1][slot] = factor
        return unit

    copies["tok"].wait()
    inputs = tok[...].astype(F32)
    normed = (inputs * row_factor(inputs)).astype(BF16)
    copies["wqs"].wait()
    for name in late:
        copies[name].start()
    put_queries(0, normed_heads(normed, wqs[:, :D], 0, (unit_q, fact_q)), scale_space)
    keys[:T] = normed_heads(normed, wqs[:, D : 2 * D], 0, (unit_k, fact_k)).astype(BF16)
    raw = dot(normed, wqs[:, 2 * D :]).astype(BF16)
    for pair in range(PAIRS):
        values[pair, :T, :128] = raw[:, lanes(pair)]
    for pair in range(PAIRS):
        grown_one[pair, :, :T] = grown(queries[0, pair], keys[:T, lanes(pair)], mask_own)
    for pair in range(PAIRS):
        partial[pair] = dot(grown_one[pair, :, :T], values[pair, :T])

    copies["cot"].wait()
    scatter(0, cot[...].astype(F32))

    for copy in near[0]:
        copy.wait_recv()
    rim = halo[...].astype(F32)
    normed = (rim * row_factor(rim)).astype(BF16)
    keys[T:] = normed_heads(normed, wqs[:, D : 2 * D], None, None).astype(BF16)
    raw = dot(normed, wqs[:, 2 * D :]).astype(BF16)
    for pair in range(PAIRS):
        values[pair, T:, :128] = raw[:, lanes(pair)]
    for pair in range(PAIRS):
        grown_one[pair, :, T:] = grown(queries[0, pair], keys[T:, lanes(pair)], mask_rim)
    for pair in range(PAIRS):
        out = partial[pair] + dot(grown_one[pair, :, T:], values[pair, T:])
        turned = 1.0 / out[:, 128:]
        inverse[0, pair] = turned
        attended[:, lanes(pair)] = paired(low, out[:, :128] * turned).astype(BF16)
    copies["wos"].wait()
    after[...] = (inputs + dot(attended[...], wos[...])).astype(BF16)
    scatter(1, after[...].astype(F32))
    table = jnp.zeros((T, 128), F32)
    for pair in range(PAIRS):
        table = jnp.where(col == 2 * pair, inverse[0, pair, :T], table)
        table = jnp.where(col == 2 * pair + 1, inverse[0, pair, T:], table)
    stats[...] = table

    upstream = collect(0)
    copies["wob"].wait()
    grad_att = dot_nt(upstream.astype(BF16), wob[...])
    for pair in range(PAIRS):
        ups_stack[pair] = stacked(grad_att[:, lanes(pair)], low)
    put_queries(2, normed_heads(normed, wqs[:, :D], None, None), scale_space)
    copies["wqb"].wait()
    for at in range(0, 3 * D, 256):
        wqb_t[at : at + 256] = wqb[:, at : at + 256].T

    rows = collect(1)
    for index in (1, 2):
        for copy in near[index]:
            copy.start()
    fact_two = row_factor(rows)
    unit_two = rows * fact_two
    normed = unit_two.astype(BF16)
    put_queries(1, normed_heads(normed, wqb[:, :D], 1, (unit_q, fact_q)), scale_band)
    keys_two[...] = normed_heads(normed, wqb[:, D : 2 * D], 1, (unit_k, fact_k)).astype(BF16)
    raw = dot(normed, wqb[:, 2 * D :]).astype(BF16)
    for pair in range(PAIRS):
        values_two[pair, :, :128] = raw[:, lanes(pair)]
    everyone = range(PAIRS)
    weight = [grown(queries[1, p], keys_two[:, lanes(p)], mask_two) for p in everyone]
    outs, turned = [], []
    for pair in everyone:
        out = dot(weight[pair], values_two[pair])
        turned.append(1.0 / out[:, 128:])
        outs.append(out[:, :128] * turned[pair])
    scatter(2, jnp.concatenate([paired(low, out) for out in outs], axis=1))
    dscore = []
    for pair in everyone:
        ups = ups_stack[pair]
        inside = inner(ups, (-ups.astype(F32) * outs[pair]).astype(BF16), values_two[pair])
        dscore.append((weight[pair].astype(F32) * (inside * turned[pair])).astype(BF16))
    for pair in everyone:
        at = lanes(pair)
        grads[:, at] = paired(low, dot(dscore[pair], keys_two[:, at])) * scale_band[:, at]
        grads[:, D + pair * 128 : D + pair * 128 + 128] = dot_tn(dscore[pair], queries[1, pair])
        wide[:, 2 * D + pair * 128 : 2 * D + pair * 128 + 128] = dot_tn(
            weight[pair], (ups_stack[pair].astype(F32) * turned[pair]).astype(BF16)
        ).astype(BF16)
    wide[:, :D] = head_back(unit_q[1], fact_q[1], grads[:, :D], ones).astype(BF16)
    wide[:, D : 2 * D] = head_back(unit_k[1], fact_k[1], grads[:, D:], ones).astype(BF16)
    back = dot(wide[...], wqb_t[...])
    scatter(3, upstream + row_back(unit_two, fact_two, back))
    for step in range(bands):
        far(step).start()

    for at in range(0, 3 * D, 256):
        wqs_t[at : at + 256] = wqs[:, at : at + 256].T
    for at in range(0, D, 256):
        wos_t[at : at + 256] = wos[:, at : at + 256].T
    for index in (1, 2):
        for copy in near[index]:
            copy.wait_recv()
    for pair in range(PAIRS):
        grown_rim[pair] = grown(queries[2, pair], keys[:T, lanes(pair)], mask_back)
        for part in range(2):
            head = 2 * pair + part
            inverse_rim[pair, part * T : part * T + T] = jnp.broadcast_to(
                stats_rim[:, head : head + 1], (T, 128)
            )

    grad_after = collect(3)
    grad_att = dot(grad_after.astype(BF16), wos_t[...])
    def stacked_ups():
        return [
            jnp.concatenate(
                [jnp.where(low, part, 0.0), jnp.where(low, 0.0, part)], axis=0
            )
            for part in (grad_att[:, lanes(pair)] for pair in range(PAIRS))
        ]

    def window_dscore(ups, weight, outs, value, turned):
        out = jnp.concatenate([outs, outs], axis=0).astype(F32)
        inside = inner(ups.astype(BF16), (-ups * out).astype(BF16), value)
        return (weight.astype(F32) * (inside * turned)).astype(BF16)

    ups_all = stacked_ups()
    dscore = []
    for pair in range(PAIRS):
        turned = inverse[0, pair]
        turned = jnp.concatenate([turned, turned], axis=1)
        dscore.append(
            window_dscore(
                ups_all[pair], grown_one[pair], attended[:, lanes(pair)], values[pair], turned
            )
        )
    for pair in range(PAIRS):
        at = lanes(pair)
        grads[:, at] = paired(low, dot(dscore[pair], keys[:, at])) * scale_space[:, at]
        partial[pair, :T, :128] = dot_tn(dscore[pair][:, :T], queries[0, pair])
        partial[pair, :T, 128:] = dot_tn(
            grown_one[pair, :, :T], (ups_all[pair] * inverse[0, pair]).astype(BF16)
        )
    wide[:, :D] = head_back(unit_q[0], fact_q[0], grads[:, :D], ones).astype(BF16)
    back = dot(wide[:, :D], wqs_t[:D])
    mixed[0] = after[...].astype(F32) + dot(collect(2).astype(BF16), wob[...])

    for sender in range(bands):
        far_arrival(sender).wait_recv()
    grad_att = dot(unpacked(got_rim[...]).astype(BF16), wos_t[...])
    ups_all = stacked_ups()
    dscore = [
        window_dscore(
            ups_all[pair],
            grown_rim[pair],
            attended_rim[:, lanes(pair)],
            values[pair, :T],
            inverse_rim[pair],
        )
        for pair in range(PAIRS)
    ]
    for pair in range(PAIRS):
        grads[:, D + pair * 128 : D + pair * 128 + 128] = partial[pair, :T, :128] + dot_tn(
            dscore[pair], queries[2, pair]
        )
        wide[:, 2 * D + pair * 128 : 2 * D + pair * 128 + 128] = (
            partial[pair, :T, 128:]
            + dot_tn(grown_rim[pair], (ups_all[pair] * inverse_rim[pair]).astype(BF16))
        ).astype(BF16)
    wide[:, D : 2 * D] = head_back(unit_k[0], fact_k[0], grads[:, D:], ones).astype(BF16)
    back = back + dot(wide[:, D:], wqs_t[D:])
    inputs = tok[...].astype(F32)
    fact_one = row_factor(inputs)
    grad[0] = grad_after + row_back(inputs * fact_one, fact_one, back)

    for index in range(3):
        for copy in near[index]:
            copy.wait_send()
    for phase in range(4):
        for step in range(1, bands):
            exchange(phase, step).wait_send()
    for step in range(bands):
        far(step).wait_send()


def deliver(mixed, grad, mixed_hbm, grad_hbm, sem):
    copies = [
        pltpu.make_async_copy(
            source.at[0, pl.ds(part * 32, 32)],
            target.at[0, pl.ds(part * 32, 32)],
            sem.at[which, part],
        )
        for part in range(4)
        for which, (source, target) in enumerate(((mixed, mixed_hbm), (grad, grad_hbm)))
    ]
    for copy in copies:
        copy.start()
    for copy in copies:
        copy.wait()


def per_device(bands, spaces, *arrays):
    kept = pltpu.VMEM((1, T, D), F32)
    vmem = pl.BlockSpec(memory_space=pltpu.VMEM)
    hbm = pl.BlockSpec(memory_space=pltpu.HBM)
    out = jax.ShapeDtypeStruct((1, T, D), F32)
    count = T // bands
    dma = pltpu.SemaphoreType.DMA
    scratch = [
        pltpu.VMEM((T, D), BF16),
        pltpu.VMEM((T, D), BF16),
        pltpu.VMEM((T, D), BF16),
        pltpu.VMEM((3, bands, T), jnp.int32),
        pltpu.SMEM((HEADS,), F32),
        pltpu.SMEM((HEADS,), F32),
        pltpu.VMEM((D, 3 * D), BF16),
        pltpu.VMEM((D, D), BF16),
        pltpu.VMEM((D, 3 * D), BF16),
        pltpu.VMEM((D, D), BF16),
        pltpu.VMEM((3 * D, D), BF16),
        pltpu.VMEM((D, D), BF16),
        pltpu.VMEM((3 * D, D), BF16),
        pltpu.VMEM((2 * T, D), BF16),
        pltpu.VMEM((PAIRS, 2 * T, 256), BF16),
        pltpu.VMEM((T, D), BF16),
        pltpu.VMEM((PAIRS, T, 256), BF16),
        pltpu.VMEM((3, PAIRS, 2 * T, 128), BF16),
        pltpu.VMEM((PAIRS, 2 * T, 128), BF16),
        pltpu.VMEM((PAIRS, 2 * T, 2 * T), BF16),
        pltpu.VMEM((PAIRS, 2 * T, T), BF16),
        pltpu.VMEM((PAIRS, 2 * T, 256), F32),
        pltpu.VMEM((1, PAIRS, 2 * T, 128), F32),
        pltpu.VMEM((PAIRS, 2 * T, 128), F32),
        pltpu.VMEM((2, T, D), F32),
        pltpu.VMEM((2, T, D), F32),
        pltpu.VMEM((2, T, D), F32),
        pltpu.VMEM((2, T, D), F32),
        pltpu.VMEM((T, 3 * D), BF16),
        pltpu.VMEM((T, D), BF16),
        pltpu.VMEM((T, D), BF16),
        pltpu.VMEM((T, D), BF16),
        pltpu.VMEM((T, 128), F32),
        pltpu.VMEM((T, 128), F32),
        pltpu.VMEM((T, 2 * D), F32),
        pltpu.VMEM((4, bands, 2 * count, HALF), BF16),
        pltpu.VMEM((4, bands, 2 * count, HALF), BF16),
        pltpu.VMEM((bands, 2 * count, HALF), BF16),
        dma((11,)),
        dma((3, 2)),
        dma((3, 2)),
        dma((4, bands)),
        dma((4, bands)),
        dma((bands,)),
        dma((bands,)),
    ]
    made = pl.pallas_call(
        functools.partial(kernel, bands, spaces),
        out_shape=(kept, kept),
        in_specs=[hbm] * 9,
        out_specs=(vmem, vmem),
        scratch_shapes=scratch,
        compiler_params=pltpu.CompilerParams(
            collective_id=0, has_side_effects=True, vmem_limit_bytes=63 * 1024 * 1024
        ),
        cost_estimate=pl.CostEstimate(
            flops=3_500_000_000, bytes_accessed=11_000_000, transcendentals=600_000
        ),
    )(*arrays)
    return pl.pallas_call(
        deliver,
        out_shape=(out, out),
        in_specs=[vmem] * 2,
        out_specs=(hbm, hbm),
        scratch_shapes=[dma((2, 4))],
    )(*[pltpu.with_memory_space_constraint(part, pltpu.VMEM) for part in made])


def solution(mesh):
    cells = P("band", "space", None)
    return jax.shard_map(
        functools.partial(per_device, mesh.shape["band"], mesh.shape["space"]),
        mesh=mesh,
        in_specs=(cells, cells, P(), P(), P(), P(), P(), P(), P()),
        out_specs=(cells, cells),
        check_vma=False,
    )
```

```python
import functools

import jax
import jax.numpy as jnp
from jax import lax
from jax.experimental import pallas as pl
from jax.experimental.pallas import tpu as pltpu
from jax.sharding import PartitionSpec as P

D = 768
HALF = D // 2
HEADS = 12
HEAD_DIM = 64
PAIRS = HEADS // 2
T = 128
RADIUS = 64
EPS = 1e-06
MESH = pl.DeviceIdType.MESH
F32 = jnp.float32
BF16 = jnp.bfloat16


def dot(left, right):
    return jnp.dot(left, right, preferred_element_type=F32)


def dot_nt(left, right):
    return lax.dot_general(left, right, (((1,), (1,)), ((), ())), preferred_element_type=F32)


def dot_tn(left, right):
    return lax.dot_general(left, right, (((0,), (0,)), ((), ())), preferred_element_type=F32)


def row_factor(values):
    return lax.rsqrt(jnp.sum(values * values, axis=-1, keepdims=True) * (1.0 / D) + EPS)


def row_back(unit, factor, upstream):
    return factor * (upstream - unit * (jnp.sum(unit * upstream, axis=-1, keepdims=True) * (1.0 / D)))


def head_means(values, ones):
    low = values.astype(BF16)
    width = ones.shape[0]
    parts = [dot(low[:, at : at + width], ones) for at in range(0, values.shape[1], width)]
    return jnp.concatenate(parts, axis=1) * (1.0 / HEAD_DIM)


def head_factor(values, ones):
    return lax.rsqrt(head_means(values * values, ones) + EPS)


def head_back(unit, factor, upstream, ones):
    return factor * (upstream - unit * head_means(unit * upstream, ones))


def stacked(pair, low):
    return jnp.concatenate([jnp.where(low, pair, 0.0), jnp.where(low, 0.0, pair)], axis=0).astype(BF16)


def lanes(pair):
    return slice(pair * 128, pair * 128 + 128)


def paired(low, stack):
    return jnp.where(low, stack[:T], stack[T:])


def grown(query_stack, keys, mask):
    scores = jnp.exp(dot_nt(query_stack, keys))
    return jnp.concatenate([scores[:T] * mask, scores[T:] * mask], axis=0).astype(BF16)


def inner(ups, outs, values_one):
    return dot_nt(jnp.concatenate([ups, outs], axis=1), values_one)


def kernel(
    bands,
    spaces,
    tok_hbm,
    cot_hbm,
    vis_hbm,
    tau_space_hbm,
    tau_band_hbm,
    wqs_hbm,
    wos_hbm,
    wqb_hbm,
    wob_hbm,
    mixed,
    grad,
    tok,
    halo,
    cot,
    vis,
    tau_space,
    tau_band,
    wqs,
    wos,
    wqb,
    wob,
    wqs_t,
    wos_t,
    wqb_t,
    keys,
    values,
    keys_two,
    values_two,
    queries,
    ups_stack,
    grown_one,
    grown_rim,
    partial,
    inverse,
    inverse_rim,
    unit_q,
    fact_q,
    unit_k,
    fact_k,
    wide,
    after,
    attended,
    attended_rim,
    stats,
    stats_rim,
    grads,
    sent,
    got,
    got_rim,
    local_sem,
    near_send,
    near_recv,
    all_send,
    all_recv,
    far_send,
    far_recv,
):
    band = lax.axis_index("band")
    space = lax.axis_index("space")
    count = T // bands
    chunk = lax.div(band, 2) + (bands // 2) * lax.rem(band, 2)
    right = lax.rem(space + 1, spaces)
    left = lax.rem(space + spaces - 1, spaces)

    def local(source, target, index):
        return pltpu.make_async_copy(source, target, local_sem.at[index])

    copies = {
        "tok": local(tok_hbm.at[0], tok, 0),
        "wqs": local(wqs_hbm, wqs, 1),
        "cot": local(cot_hbm.at[0], cot, 2),
        "wos": local(wos_hbm, wos, 3),
        "wob": local(wob_hbm, wob, 4),
        "wqb": local(wqb_hbm, wqb, 5),
        "tau_space": local(tau_space_hbm, tau_space, 9),
        "tau_band": local(tau_band_hbm, tau_band, 10),
    }
    for index, block in enumerate((left, space, right)):
        copies["vis%d" % index] = local(
            vis_hbm.at[:, pl.ds(pl.multiple_of(block * T, T), T)], vis.at[index], 6 + index
        )
    early = ("tok", "cot", "vis0", "vis1", "vis2", "tau_space", "tau_band", "wqs")
    late = ("wob", "wos", "wqb")
    for name in early:
        copies[name].start()

    barrier = pltpu.get_barrier_semaphore()
    for other in (left, right):
        pl.semaphore_signal(barrier, inc=1, device_id=(band, other), device_id_type=MESH)
    for step in range(1, bands):
        pl.semaphore_signal(
            barrier,
            inc=1,
            device_id=(lax.rem(band + step, bands), space),
            device_id_type=MESH,
        )
    pl.semaphore_wait(barrier, bands + 1)

    def neighbours(source, target, index):
        return [
            pltpu.make_async_remote_copy(
                src_ref=source.at[pl.ds(at, RADIUS)],
                dst_ref=target.at[pl.ds(at, RADIUS)],
                send_sem=near_send.at[index, side],
                recv_sem=near_recv.at[index, side],
                device_id=(band, other),
                device_id_type=MESH,
            )
            for side, at, other in ((0, RADIUS, right), (1, 0, left))
        ]

    near = [
        neighbours(tok_hbm.at[0], halo, 0),
        neighbours(attended, attended_rim, 1),
        neighbours(stats, stats_rim, 2),
    ]
    for copy in near[0]:
        copy.start()

    def exchange(phase, step):
        other = lax.rem(band + step, bands)
        away = lax.div(other, 2) + (bands // 2) * lax.rem(other, 2)
        return pltpu.make_async_remote_copy(
            src_ref=sent.at[phase, away if phase < 2 else other],
            dst_ref=got.at[phase, band if phase < 2 else chunk],
            send_sem=all_send.at[phase],
            recv_sem=all_recv.at[phase],
            device_id=(other, space),
            device_id_type=MESH,
        )

    def whole(phase):
        return pltpu.make_async_remote_copy(
            src_ref=sent.at[phase, pl.ds(0, bands - 1)],
            dst_ref=got.at[phase, pl.ds(0, bands - 1)],
            send_sem=all_send.at[phase],
            recv_sem=all_recv.at[phase],
            device_id=(lax.rem(band + 1, bands), space),
            device_id_type=MESH,
        )

    def scatter(phase, rows):
        pieces = [
            rows[:, :HALF].reshape(bands, count, HALF),
            rows[:, HALF:].reshape(bands, count, HALF),
        ]
        sent[phase] = jnp.concatenate(pieces, axis=1).astype(BF16)
        for step in range(1, bands):
            exchange(phase, step).start()
        if phase < 2:
            got[phase, band] = sent[phase, chunk]
        else:
            got[phase, chunk] = sent[phase, band]

    def unpacked(slots):
        rows = slots.astype(F32)
        return jnp.concatenate(
            [rows[:, :count].reshape(T, HALF), rows[:, count:].reshape(T, HALF)], axis=1
        )

    def collect(phase):
        whole(phase).wait_recv()
        return unpacked(got[phase])

    toward = lax.rem(space + spaces - 1 + 2 * lax.rem(band, 2), spaces)

    def far(step):
        other = lax.rem(band + step, bands)
        return pltpu.make_async_remote_copy(
            src_ref=sent.at[3, other],
            dst_ref=got_rim.at[chunk],
            send_sem=far_send,
            recv_sem=far_recv,
            device_id=(other, toward),
            device_id_type=MESH,
        )

    far_whole = pltpu.make_async_remote_copy(
        src_ref=sent.at[3],
        dst_ref=got_rim,
        send_sem=far_send,
        recv_sem=far_recv,
        device_id=(band, toward),
        device_id_type=MESH,
    )

    low = lax.broadcasted_iota(jnp.int32, (T, 128), 1) < HEAD_DIM
    ones = jnp.where(
        (lax.broadcasted_iota(jnp.int32, (256, 256), 0) >> 6)
        == (lax.broadcasted_iota(jnp.int32, (256, 256), 1) >> 6),
        1.0,
        0.0,
    ).astype(BF16)
    for pair in range(PAIRS):
        values[pair, :, 128:] = jnp.ones((2 * T, 128), BF16)
        values_two[pair, :, 128:] = jnp.ones((T, 128), BF16)

    for index in range(3):
        copies["vis%d" % index].wait()
    group = lax.broadcasted_iota(jnp.int32, (bands, 128), 0)
    lane = lax.broadcasted_iota(jnp.int32, (bands, 128), 1)

    def own_row(index):
        return jnp.sum(jnp.where(group == band, vis[index], 0), axis=0, keepdims=True)

    row = lax.broadcasted_iota(jnp.int32, (T, T), 0)
    col = lax.broadcasted_iota(jnp.int32, (T, T), 1)
    own_seen = own_row(1) == 1
    rim_seen = jnp.where(lane[:1] < RADIUS, own_row(2), own_row(0)) == 1

    def within(offset):
        return (offset >= -RADIUS) & (offset <= RADIUS)

    def flag(test):
        return jnp.where(test, 1.0, 0.0)

    mask_own = flag(within(row - col) & (own_seen | (row == col)))
    mask_rim = flag(within(jnp.where(col < RADIUS, col + T, col - T) - row) & rim_seen)
    mask_back = flag(within(jnp.where(row < RADIUS, row + T, row - T) - col) & own_seen)
    pick = flag(row == chunk * count + lax.rem(col, count))
    spread = dot(vis[1].astype(F32), pick)
    seen = jnp.sum(
        jnp.where(group == lax.div(lane, count), spread, 0.0), axis=0, keepdims=True
    )
    same = lax.rem(row, count) == lax.rem(col, count)
    mask_two = flag(same & ((seen > 0.5) | (row == col)))

    copies["tau_space"].wait()
    copies["tau_band"].wait()

    def scale_row(tau):
        pieces = [
            jnp.where(low[:1], tau[2 * pair], tau[2 * pair + 1]) * (1.0 / HEAD_DIM)
            for pair in range(PAIRS)
        ]
        return jnp.concatenate(pieces, axis=1)

    scale_space = scale_row(tau_space)
    scale_band = scale_row(tau_band)

    def put_queries(slot, unit, scale):
        scaled = unit * scale
        for pair in range(PAIRS):
            queries[slot, pair] = stacked(scaled[:, lanes(pair)], low)

    def normed_heads(normed, weight, slot, which):
        raw = dot(normed, weight)
        factor = head_factor(raw, ones)
        unit = raw * factor
        if which is not None:
            which[0][slot] = unit
            which[1][slot] = factor
        return unit

    copies["tok"].wait()
    inputs = tok[...].astype(F32)
    normed = (inputs * row_factor(inputs)).astype(BF16)
    copies["wqs"].wait()
    for name in late:
        copies[name].start()
    put_queries(0, normed_heads(normed, wqs[:, :D], 0, (unit_q, fact_q)), scale_space)
    keys[:T] = normed_heads(normed, wqs[:, D : 2 * D], 0, (unit_k, fact_k)).astype(BF16)
    raw = dot(normed, wqs[:, 2 * D :]).astype(BF16)
    for pair in range(PAIRS):
        values[pair, :T, :128] = raw[:, lanes(pair)]
    for pair in range(PAIRS):
        grown_one[pair, :, :T] = grown(queries[0, pair], keys[:T, lanes(pair)], mask_own)
    for pair in range(PAIRS):
        partial[pair] = dot(grown_one[pair, :, :T], values[pair, :T])

    copies["cot"].wait()
    scatter(0, cot[...].astype(F32))

    for copy in near[0]:
        copy.wait_recv()
    rim = halo[...].astype(F32)
    normed = (rim * row_factor(rim)).astype(BF16)
    keys[T:] = normed_heads(normed, wqs[:, D : 2 * D], None, None).astype(BF16)
    raw = dot(normed, wqs[:, 2 * D :]).astype(BF16)
    for pair in range(PAIRS):
        values[pair, T:, :128] = raw[:, lanes(pair)]
    for pair in range(PAIRS):
        grown_one[pair, :, T:] = grown(queries[0, pair], keys[T:, lanes(pair)], mask_rim)
    for pair in range(PAIRS):
        out = partial[pair] + dot(grown_one[pair, :, T:], values[pair, T:])
        turned = 1.0 / out[:, 128:]
        inverse[0, pair] = turned
        attended[:, lanes(pair)] = paired(low, out[:, :128] * turned).astype(BF16)
    copies["wos"].wait()
    after[...] = (inputs + dot(attended[...], wos[...])).astype(BF16)
    scatter(1, after[...].astype(F32))
    table = jnp.zeros((T, 128), F32)
    for pair in range(PAIRS):
        table = jnp.where(col == 2 * pair, inverse[0, pair, :T], table)
        table = jnp.where(col == 2 * pair + 1, inverse[0, pair, T:], table)
    stats[...] = table

    upstream = collect(0)
    copies["wob"].wait()
    grad_att = dot_nt(upstream.astype(BF16), wob[...])
    for pair in range(PAIRS):
        ups_stack[pair] = stacked(grad_att[:, lanes(pair)], low)
    put_queries(2, normed_heads(normed, wqs[:, :D], None, None), scale_space)
    copies["wqb"].wait()
    for at in range(0, 3 * D, 256):
        wqb_t[at : at + 256] = wqb[:, at : at + 256].T

    rows = collect(1)
    for index in (1, 2):
        for copy in near[index]:
            copy.start()
    fact_two = row_factor(rows)
    unit_two = rows * fact_two
    normed = unit_two.astype(BF16)
    put_queries(1, normed_heads(normed, wqb[:, :D], 1, (unit_q, fact_q)), scale_band)
    keys_two[...] = normed_heads(normed, wqb[:, D : 2 * D], 1, (unit_k, fact_k)).astype(BF16)
    raw = dot(normed, wqb[:, 2 * D :]).astype(BF16)
    for pair in range(PAIRS):
        values_two[pair, :, :128] = raw[:, lanes(pair)]
    everyone = range(PAIRS)
    weight = [grown(queries[1, p], keys_two[:, lanes(p)], mask_two) for p in everyone]
    outs, turned = [], []
    for pair in everyone:
        out = dot(weight[pair], values_two[pair])
        turned.append(1.0 / out[:, 128:])
        outs.append(out[:, :128] * turned[pair])
    scatter(2, jnp.concatenate([paired(low, out) for out in outs], axis=1))
    dscore = []
    for pair in everyone:
        ups = ups_stack[pair]
        inside = inner(ups, (-ups.astype(F32) * outs[pair]).astype(BF16), values_two[pair])
        dscore.append((weight[pair].astype(F32) * (inside * turned[pair])).astype(BF16))
    for pair in everyone:
        at = lanes(pair)
        grads[:, at] = paired(low, dot(dscore[pair], keys_two[:, at])) * scale_band[:, at]
        grads[:, D + pair * 128 : D + pair * 128 + 128] = dot_tn(dscore[pair], queries[1, pair])
        wide[:, 2 * D + pair * 128 : 2 * D + pair * 128 + 128] = dot_tn(
            weight[pair], (ups_stack[pair].astype(F32) * turned[pair]).astype(BF16)
        ).astype(BF16)
    wide[:, :D] = head_back(unit_q[1], fact_q[1], grads[:, :D], ones).astype(BF16)
    wide[:, D : 2 * D] = head_back(unit_k[1], fact_k[1], grads[:, D:], ones).astype(BF16)
    back = dot(wide[...], wqb_t[...])
    scatter(3, upstream + row_back(unit_two, fact_two, back))
    for step in range(bands):
        far(step).start()

    for at in range(0, 3 * D, 256):
        wqs_t[at : at + 256] = wqs[:, at : at + 256].T
    for at in range(0, D, 256):
        wos_t[at : at + 256] = wos[:, at : at + 256].T
    for index in (1, 2):
        for copy in near[index]:
            copy.wait_recv()
    for pair in range(PAIRS):
        grown_rim[pair] = grown(queries[2, pair], keys[:T, lanes(pair)], mask_back)
        for part in range(2):
            head = 2 * pair + part
            inverse_rim[pair, part * T : part * T + T] = jnp.broadcast_to(
                stats_rim[:, head : head + 1], (T, 128)
            )

    grad_after = collect(3)
    grad_att = dot(grad_after.astype(BF16), wos_t[...])
    def stacked_ups():
        return [
            jnp.concatenate(
                [jnp.where(low, part, 0.0), jnp.where(low, 0.0, part)], axis=0
            )
            for part in (grad_att[:, lanes(pair)] for pair in range(PAIRS))
        ]

    def window_dscore(ups, weight, outs, value, turned):
        out = jnp.concatenate([outs, outs], axis=0).astype(F32)
        inside = inner(ups.astype(BF16), (-ups * out).astype(BF16), value)
        return (weight.astype(F32) * (inside * turned)).astype(BF16)

    ups_all = stacked_ups()
    dscore = []
    for pair in range(PAIRS):
        turned = inverse[0, pair]
        turned = jnp.concatenate([turned, turned], axis=1)
        dscore.append(
            window_dscore(
                ups_all[pair], grown_one[pair], attended[:, lanes(pair)], values[pair], turned
            )
        )
    for pair in range(PAIRS):
        at = lanes(pair)
        grads[:, at] = paired(low, dot(dscore[pair], keys[:, at])) * scale_space[:, at]
        partial[pair, :T, :128] = dot_tn(dscore[pair][:, :T], queries[0, pair])
        partial[pair, :T, 128:] = dot_tn(
            grown_one[pair, :, :T], (ups_all[pair] * inverse[0, pair]).astype(BF16)
        )
    wide[:, :D] = head_back(unit_q[0], fact_q[0], grads[:, :D], ones).astype(BF16)
    back = dot(wide[:, :D], wqs_t[:D])
    mixed[0] = after[...].astype(F32) + dot(collect(2).astype(BF16), wob[...])

    for index in range(3):
        for copy in near[index]:
            copy.wait_send()
    for phase in range(4):
        whole(phase).wait_send()
    far_whole.wait_recv()
    grad_att = dot(unpacked(got_rim[...]).astype(BF16), wos_t[...])
    ups_all = stacked_ups()
    dscore = [
        window_dscore(
            ups_all[pair],
            grown_rim[pair],
            attended_rim[:, lanes(pair)],
            values[pair, :T],
            inverse_rim[pair],
        )
        for pair in range(PAIRS)
    ]
    for pair in range(PAIRS):
        grads[:, D + pair * 128 : D + pair * 128 + 128] = partial[pair, :T, :128] + dot_tn(
            dscore[pair], queries[2, pair]
        )
        wide[:, 2 * D + pair * 128 : 2 * D + pair * 128 + 128] = (
            partial[pair, :T, 128:]
            + dot_tn(grown_rim[pair], (ups_all[pair] * inverse_rim[pair]).astype(BF16))
        ).astype(BF16)
    wide[:, D : 2 * D] = head_back(unit_k[0], fact_k[0], grads[:, D:], ones).astype(BF16)
    back = back + dot(wide[:, D:], wqs_t[D:])
    inputs = tok[...].astype(F32)
    fact_one = row_factor(inputs)
    grad[0] = grad_after + row_back(inputs * fact_one, fact_one, back)

    far_whole.wait_send()


def deliver(mixed, grad, mixed_hbm, grad_hbm, sem):
    copies = [
        pltpu.make_async_copy(
            source.at[0, pl.ds(part * 32, 32)],
            target.at[0, pl.ds(part * 32, 32)],
            sem.at[which, part],
        )
        for part in range(4)
        for which, (source, target) in enumerate(((mixed, mixed_hbm), (grad, grad_hbm)))
    ]
    for copy in copies:
        copy.start()
    for copy in copies:
        copy.wait()


def per_device(bands, spaces, *arrays):
    kept = pltpu.VMEM((1, T, D), F32)
    vmem = pl.BlockSpec(memory_space=pltpu.VMEM)
    hbm = pl.BlockSpec(memory_space=pltpu.HBM)
    out = jax.ShapeDtypeStruct((1, T, D), F32)
    count = T // bands
    dma = pltpu.SemaphoreType.DMA
    scratch = [
        pltpu.VMEM((T, D), BF16),
        pltpu.VMEM((T, D), BF16),
        pltpu.VMEM((T, D), BF16),
        pltpu.VMEM((3, bands, T), jnp.int32),
        pltpu.SMEM((HEADS,), F32),
        pltpu.SMEM((HEADS,), F32),
        pltpu.VMEM((D, 3 * D), BF16),
        pltpu.VMEM((D, D), BF16),
        pltpu.VMEM((D, 3 * D), BF16),
        pltpu.VMEM((D, D), BF16),
        pltpu.VMEM((3 * D, D), BF16),
        pltpu.VMEM((D, D), BF16),
        pltpu.VMEM((3 * D, D), BF16),
        pltpu.VMEM((2 * T, D), BF16),
        pltpu.VMEM((PAIRS, 2 * T, 256), BF16),
        pltpu.VMEM((T, D), BF16),
        pltpu.VMEM((PAIRS, T, 256), BF16),
        pltpu.VMEM((3, PAIRS, 2 * T, 128), BF16),
        pltpu.VMEM((PAIRS, 2 * T, 128), BF16),
        pltpu.VMEM((PAIRS, 2 * T, 2 * T), BF16),
        pltpu.VMEM((PAIRS, 2 * T, T), BF16),
        pltpu.VMEM((PAIRS, 2 * T, 256), F32),
        pltpu.VMEM((1, PAIRS, 2 * T, 128), F32),
        pltpu.VMEM((PAIRS, 2 * T, 128), F32),
        pltpu.VMEM((2, T, D), F32),
        pltpu.VMEM((2, T, D), F32),
        pltpu.VMEM((2, T, D), F32),
        pltpu.VMEM((2, T, D), F32),
        pltpu.VMEM((T, 3 * D), BF16),
        pltpu.VMEM((T, D), BF16),
        pltpu.VMEM((T, D), BF16),
        pltpu.VMEM((T, D), BF16),
        pltpu.VMEM((T, 128), F32),
        pltpu.VMEM((T, 128), F32),
        pltpu.VMEM((T, 2 * D), F32),
        pltpu.VMEM((4, bands, 2 * count, HALF), BF16),
        pltpu.VMEM((4, bands, 2 * count, HALF), BF16),
        pltpu.VMEM((bands, 2 * count, HALF), BF16),
        dma((11,)),
        dma((3, 2)),
        dma((3, 2)),
        dma((4,)),
        dma((4,)),
        dma,
        dma,
    ]
    made = pl.pallas_call(
        functools.partial(kernel, bands, spaces),
        out_shape=(kept, kept),
        in_specs=[hbm] * 9,
        out_specs=(vmem, vmem),
        scratch_shapes=scratch,
        compiler_params=pltpu.CompilerParams(
            collective_id=0, has_side_effects=True, vmem_limit_bytes=63 * 1024 * 1024
        ),
        cost_estimate=pl.CostEstimate(
            flops=3_500_000_000, bytes_accessed=11_000_000, transcendentals=600_000
        ),
    )(*arrays)
    return pl.pallas_call(
        deliver,
        out_shape=(out, out),
        in_specs=[vmem] * 2,
        out_specs=(hbm, hbm),
        scratch_shapes=[dma((2, 4))],
    )(*[pltpu.with_memory_space_constraint(part, pltpu.VMEM) for part in made])


def solution(mesh):
    cells = P("band", "space", None)
    return jax.shard_map(
        functools.partial(per_device, mesh.shape["band"], mesh.shape["space"]),
        mesh=mesh,
        in_specs=(cells, cells, P(), P(), P(), P(), P(), P(), P()),
        out_specs=(cells, cells),
        check_vma=False,
    )
```

```python
import functools

import jax
import jax.numpy as jnp
from jax import lax
from jax.experimental import pallas as pl
from jax.experimental.pallas import tpu as pltpu
from jax.sharding import PartitionSpec as P

D = 768
HALF = D // 2
HEADS = 12
HEAD_DIM = 64
PAIRS = HEADS // 2
T = 128
RADIUS = 64
EPS = 1e-06
MESH = pl.DeviceIdType.MESH
F32 = jnp.float32
BF16 = jnp.bfloat16


def dot(left, right):
    return jnp.dot(left, right, preferred_element_type=F32)


def dot_nt(left, right):
    return lax.dot_general(left, right, (((1,), (1,)), ((), ())), preferred_element_type=F32)


def dot_tn(left, right):
    return lax.dot_general(left, right, (((0,), (0,)), ((), ())), preferred_element_type=F32)


def row_factor(values):
    return lax.rsqrt(jnp.sum(values * values, axis=-1, keepdims=True) * (1.0 / D) + EPS)


def row_back(unit, factor, upstream):
    return factor * (upstream - unit * (jnp.sum(unit * upstream, axis=-1, keepdims=True) * (1.0 / D)))


def head_means(values, ones):
    low = values.astype(BF16)
    width = ones.shape[0]
    parts = [dot(low[:, at : at + width], ones) for at in range(0, values.shape[1], width)]
    return jnp.concatenate(parts, axis=1) * (1.0 / HEAD_DIM)


def head_factor(values, ones):
    return lax.rsqrt(head_means(values * values, ones) + EPS)


def head_back(unit, factor, upstream, ones):
    return factor * (upstream - unit * head_means(unit * upstream, ones))


def stacked(pair, low):
    return jnp.concatenate([jnp.where(low, pair, 0.0), jnp.where(low, 0.0, pair)], axis=0).astype(BF16)


def lanes(pair):
    return slice(pair * 128, pair * 128 + 128)


def paired(low, stack):
    return jnp.where(low, stack[:T], stack[T:])


def grown(query_stack, keys, mask):
    scores = jnp.exp(dot_nt(query_stack, keys))
    return jnp.concatenate([scores[:T] * mask, scores[T:] * mask], axis=0).astype(BF16)


def inner(ups, outs, values_one):
    return dot_nt(jnp.concatenate([ups, outs], axis=1), values_one)


def kernel(
    bands,
    spaces,
    tok_hbm,
    cot_hbm,
    vis_hbm,
    tau_space_hbm,
    tau_band_hbm,
    wqs_hbm,
    wos_hbm,
    wqb_hbm,
    wob_hbm,
    mixed,
    grad,
    tok,
    halo,
    cot,
    vis,
    tau_space,
    tau_band,
    wqs,
    wos,
    wqb,
    wob,
    wqs_t,
    wos_t,
    wqb_t,
    keys,
    values,
    keys_two,
    values_two,
    queries,
    ups_stack,
    grown_one,
    grown_rim,
    partial,
    inverse,
    inverse_rim,
    unit_q,
    fact_q,
    unit_k,
    fact_k,
    wide,
    after,
    attended,
    attended_rim,
    stats,
    stats_rim,
    grads,
    sent,
    got,
    got_rim,
    sent_four,
    got_four,
    sent_two,
    got_two,
    local_sem,
    near_send,
    near_recv,
    all_send,
    all_recv,
    far_send,
    far_recv,
):
    band = lax.axis_index("band")
    space = lax.axis_index("space")
    count = T // bands
    chunk = lax.div(band, 2) + (bands // 2) * lax.rem(band, 2)
    right = lax.rem(space + 1, spaces)
    left = lax.rem(space + spaces - 1, spaces)

    def local(source, target, index):
        return pltpu.make_async_copy(source, target, local_sem.at[index])

    copies = {
        "tok": local(tok_hbm.at[0], tok, 0),
        "wqs": local(wqs_hbm, wqs, 1),
        "cot": local(cot_hbm.at[0], cot, 2),
        "wos": local(wos_hbm, wos, 3),
        "wob": local(wob_hbm, wob, 4),
        "wqb": local(wqb_hbm, wqb, 5),
        "tau_space": local(tau_space_hbm, tau_space, 9),
        "tau_band": local(tau_band_hbm, tau_band, 10),
    }
    for index, block in enumerate((left, space, right)):
        copies["vis%d" % index] = local(
            vis_hbm.at[:, pl.ds(pl.multiple_of(block * T, T), T)], vis.at[index], 6 + index
        )
    early = ("tok", "cot", "vis0", "vis1", "vis2", "tau_space", "tau_band", "wqs")
    late = ("wob", "wos", "wqb")
    for name in early:
        copies[name].start()

    barrier = pltpu.get_barrier_semaphore()
    for other in (left, right):
        pl.semaphore_signal(barrier, inc=1, device_id=(band, other), device_id_type=MESH)
    for step in range(1, bands):
        pl.semaphore_signal(
            barrier,
            inc=1,
            device_id=(lax.rem(band + step, bands), space),
            device_id_type=MESH,
        )
    pl.semaphore_wait(barrier, bands + 1)

    def neighbours(source, target, index):
        return [
            pltpu.make_async_remote_copy(
                src_ref=source.at[pl.ds(at, RADIUS)],
                dst_ref=target.at[pl.ds(at, RADIUS)],
                send_sem=near_send.at[index, side],
                recv_sem=near_recv.at[index, side],
                device_id=(band, other),
                device_id_type=MESH,
            )
            for side, at, other in ((0, RADIUS, right), (1, 0, left))
        ]

    near = [
        neighbours(tok_hbm.at[0], halo, 0),
        neighbours(attended, attended_rim, 1),
        neighbours(stats, stats_rim, 2),
    ]
    for copy in near[0]:
        copy.start()

    outbox = [sent.at[0], sent.at[1], sent.at[2], sent_four, sent_two]
    inbox = [got.at[0], got.at[1], got.at[2], got_four, got_two]

    def exchange(phase, step):
        other = lax.rem(band + step, bands)
        away = lax.div(other, 2) + (bands // 2) * lax.rem(other, 2)
        return pltpu.make_async_remote_copy(
            src_ref=outbox[phase].at[away if phase < 2 else other],
            dst_ref=inbox[phase].at[band if phase < 2 else chunk],
            send_sem=all_send.at[phase],
            recv_sem=all_recv.at[phase],
            device_id=(other, space),
            device_id_type=MESH,
        )

    def whole(phase):
        return pltpu.make_async_remote_copy(
            src_ref=outbox[phase].at[pl.ds(0, bands - 1)],
            dst_ref=inbox[phase].at[pl.ds(0, bands - 1)],
            send_sem=all_send.at[phase],
            recv_sem=all_recv.at[phase],
            device_id=(lax.rem(band + 1, bands), space),
            device_id_type=MESH,
        )

    def scatter(phase, rows):
        half = rows.shape[1] // 2
        pieces = [
            rows[:, :half].reshape(bands, count, half),
            rows[:, half:].reshape(bands, count, half),
        ]
        outbox[phase][...] = jnp.concatenate(pieces, axis=1).astype(BF16)
        for step in range(1, bands):
            exchange(phase, step).start()
        if phase < 2:
            inbox[phase][band] = outbox[phase][chunk]
        else:
            inbox[phase][chunk] = outbox[phase][band]

    def unpacked(slots):
        rows = slots.astype(F32)
        half = rows.shape[2]
        return jnp.concatenate(
            [rows[:, :count].reshape(T, half), rows[:, count:].reshape(T, half)], axis=1
        )

    def collect(phase):
        whole(phase).wait_recv()
        return unpacked(inbox[phase][...])

    toward = lax.rem(space + spaces - 1 + 2 * lax.rem(band, 2), spaces)

    def far(step):
        other = lax.rem(band + step, bands)
        return pltpu.make_async_remote_copy(
            src_ref=sent.at[2, other],
            dst_ref=got_rim.at[chunk],
            send_sem=far_send,
            recv_sem=far_recv,
            device_id=(other, toward),
            device_id_type=MESH,
        )

    far_whole = pltpu.make_async_remote_copy(
        src_ref=sent.at[2],
        dst_ref=got_rim,
        send_sem=far_send,
        recv_sem=far_recv,
        device_id=(band, toward),
        device_id_type=MESH,
    )

    low = lax.broadcasted_iota(jnp.int32, (T, 128), 1) < HEAD_DIM
    ones = jnp.where(
        (lax.broadcasted_iota(jnp.int32, (256, 256), 0) >> 6)
        == (lax.broadcasted_iota(jnp.int32, (256, 256), 1) >> 6),
        1.0,
        0.0,
    ).astype(BF16)
    for pair in range(PAIRS):
        values[pair, :, 128:] = jnp.ones((2 * T, 128), BF16)
        values_two[pair, :, 128:] = jnp.ones((T, 128), BF16)

    for index in range(3):
        copies["vis%d" % index].wait()
    group = lax.broadcasted_iota(jnp.int32, (bands, 128), 0)
    lane = lax.broadcasted_iota(jnp.int32, (bands, 128), 1)

    def own_row(index):
        return jnp.sum(jnp.where(group == band, vis[index], 0), axis=0, keepdims=True)

    row = lax.broadcasted_iota(jnp.int32, (T, T), 0)
    col = lax.broadcasted_iota(jnp.int32, (T, T), 1)
    own_seen = own_row(1) == 1
    rim_seen = jnp.where(lane[:1] < RADIUS, own_row(2), own_row(0)) == 1

    def within(offset):
        return (offset >= -RADIUS) & (offset <= RADIUS)

    def flag(test):
        return jnp.where(test, 1.0, 0.0)

    mask_own = flag(within(row - col) & (own_seen | (row == col)))
    mask_rim = flag(within(jnp.where(col < RADIUS, col + T, col - T) - row) & rim_seen)
    mask_back = flag(within(jnp.where(row < RADIUS, row + T, row - T) - col) & own_seen)
    pick = flag(row == chunk * count + lax.rem(col, count))
    spread = dot(vis[1].astype(F32), pick)
    seen = jnp.sum(
        jnp.where(group == lax.div(lane, count), spread, 0.0), axis=0, keepdims=True
    )
    same = lax.rem(row, count) == lax.rem(col, count)
    mask_two = flag(same & ((seen > 0.5) | (row == col)))

    copies["tau_space"].wait()
    copies["tau_band"].wait()

    def scale_row(tau):
        pieces = [
            jnp.where(low[:1], tau[2 * pair], tau[2 * pair + 1]) * (1.0 / HEAD_DIM)
            for pair in range(PAIRS)
        ]
        return jnp.concatenate(pieces, axis=1)

    scale_space = scale_row(tau_space)
    scale_band = scale_row(tau_band)

    def put_queries(slot, unit, scale):
        scaled = unit * scale
        for pair in range(PAIRS):
            queries[slot, pair] = stacked(scaled[:, lanes(pair)], low)

    def normed_heads(normed, weight, slot, which):
        raw = dot(normed, weight)
        factor = head_factor(raw, ones)
        unit = raw * factor
        if which is not None:
            which[0][slot] = unit
            which[1][slot] = factor
        return unit

    copies["tok"].wait()
    inputs = tok[...].astype(F32)
    normed = (inputs * row_factor(inputs)).astype(BF16)
    copies["wqs"].wait()
    for name in late:
        copies[name].start()
    put_queries(0, normed_heads(normed, wqs[:, :D], 0, (unit_q, fact_q)), scale_space)
    keys[:T] = normed_heads(normed, wqs[:, D : 2 * D], 0, (unit_k, fact_k)).astype(BF16)
    raw = dot(normed, wqs[:, 2 * D :]).astype(BF16)
    for pair in range(PAIRS):
        values[pair, :T, :128] = raw[:, lanes(pair)]
    for pair in range(PAIRS):
        grown_one[pair, :, :T] = grown(queries[0, pair], keys[:T, lanes(pair)], mask_own)
    for pair in range(PAIRS):
        partial[pair] = dot(grown_one[pair, :, :T], values[pair, :T])

    copies["cot"].wait()
    scatter(0, cot[...].astype(F32))

    for copy in near[0]:
        copy.wait_recv()
    rim = halo[...].astype(F32)
    normed = (rim * row_factor(rim)).astype(BF16)
    keys[T:] = normed_heads(normed, wqs[:, D : 2 * D], None, None).astype(BF16)
    raw = dot(normed, wqs[:, 2 * D :]).astype(BF16)
    for pair in range(PAIRS):
        values[pair, T:, :128] = raw[:, lanes(pair)]
    for pair in range(PAIRS):
        grown_one[pair, :, T:] = grown(queries[0, pair], keys[T:, lanes(pair)], mask_rim)
    for pair in range(PAIRS):
        out = partial[pair] + dot(grown_one[pair, :, T:], values[pair, T:])
        turned = 1.0 / out[:, 128:]
        inverse[0, pair] = turned
        attended[:, lanes(pair)] = paired(low, out[:, :128] * turned).astype(BF16)
    copies["wos"].wait()
    after[...] = (inputs + dot(attended[...], wos[...])).astype(BF16)
    scatter(1, after[...].astype(F32))
    table = jnp.zeros((T, 128), F32)
    for pair in range(PAIRS):
        table = jnp.where(col == 2 * pair, inverse[0, pair, :T], table)
        table = jnp.where(col == 2 * pair + 1, inverse[0, pair, T:], table)
    stats[...] = table

    upstream = collect(0)
    copies["wob"].wait()
    grad_att = dot_nt(upstream.astype(BF16), wob[...])
    for pair in range(PAIRS):
        ups_stack[pair] = stacked(grad_att[:, lanes(pair)], low)
    put_queries(2, normed_heads(normed, wqs[:, :D], None, None), scale_space)
    copies["wqb"].wait()
    for at in range(0, 3 * D, 256):
        wqb_t[at : at + 256] = wqb[:, at : at + 256].T

    for index in (1, 2):
        for copy in near[index]:
            copy.start()
    rows = collect(1)
    fact_two = row_factor(rows)
    unit_two = rows * fact_two
    normed = unit_two.astype(BF16)
    put_queries(1, normed_heads(normed, wqb[:, :D], 1, (unit_q, fact_q)), scale_band)
    keys_two[...] = normed_heads(normed, wqb[:, D : 2 * D], 1, (unit_k, fact_k)).astype(BF16)
    raw = dot(normed, wqb[:, 2 * D :]).astype(BF16)
    for pair in range(PAIRS):
        values_two[pair, :, :128] = raw[:, lanes(pair)]
    everyone = range(PAIRS)
    weight = [grown(queries[1, p], keys_two[:, lanes(p)], mask_two) for p in everyone]
    outs, turned = [], []
    for pair in everyone:
        out = dot(weight[pair], values_two[pair])
        turned.append(1.0 / out[:, 128:])
        outs.append(out[:, :128] * turned[pair])
    scatter(3, jnp.concatenate([paired(low, out) for out in outs[:4]], axis=1))
    dscore = []
    for pair in everyone:
        ups = ups_stack[pair]
        inside = inner(ups, (-ups.astype(F32) * outs[pair]).astype(BF16), values_two[pair])
        dscore.append((weight[pair].astype(F32) * (inside * turned[pair])).astype(BF16))
    for pair in everyone:
        at = lanes(pair)
        grads[:, at] = paired(low, dot(dscore[pair], keys_two[:, at])) * scale_band[:, at]
        grads[:, D + pair * 128 : D + pair * 128 + 128] = dot_tn(dscore[pair], queries[1, pair])
        wide[:, 2 * D + pair * 128 : 2 * D + pair * 128 + 128] = dot_tn(
            weight[pair], (ups_stack[pair].astype(F32) * turned[pair]).astype(BF16)
        ).astype(BF16)
    wide[:, :D] = head_back(unit_q[1], fact_q[1], grads[:, :D], ones).astype(BF16)
    wide[:, D : 2 * D] = head_back(unit_k[1], fact_k[1], grads[:, D:], ones).astype(BF16)
    back = dot(wide[...], wqb_t[...])
    scatter(2, upstream + row_back(unit_two, fact_two, back))
    for step in range(bands):
        far(step).start()
    scatter(4, jnp.concatenate([paired(low, out) for out in outs[4:]], axis=1))

    for at in range(0, 3 * D, 256):
        wqs_t[at : at + 256] = wqs[:, at : at + 256].T
    for at in range(0, D, 256):
        wos_t[at : at + 256] = wos[:, at : at + 256].T
    for pair in range(PAIRS):
        grown_rim[pair] = grown(queries[2, pair], keys[:T, lanes(pair)], mask_back)

    grad_after = collect(2)
    grad_att = dot(grad_after.astype(BF16), wos_t[...])
    def stacked_ups():
        return [
            jnp.concatenate(
                [jnp.where(low, part, 0.0), jnp.where(low, 0.0, part)], axis=0
            )
            for part in (grad_att[:, lanes(pair)] for pair in range(PAIRS))
        ]

    def window_dscore(ups, weight, outs, value, turned):
        out = jnp.concatenate([outs, outs], axis=0).astype(F32)
        inside = inner(ups.astype(BF16), (-ups * out).astype(BF16), value)
        return (weight.astype(F32) * (inside * turned)).astype(BF16)

    ups_all = stacked_ups()
    dscore = []
    for pair in range(PAIRS):
        turned = inverse[0, pair]
        turned = jnp.concatenate([turned, turned], axis=1)
        dscore.append(
            window_dscore(
                ups_all[pair], grown_one[pair], attended[:, lanes(pair)], values[pair], turned
            )
        )
    for pair in range(PAIRS):
        at = lanes(pair)
        grads[:, at] = paired(low, dot(dscore[pair], keys[:, at])) * scale_space[:, at]
        partial[pair, :T, :128] = dot_tn(dscore[pair][:, :T], queries[0, pair])
        partial[pair, :T, 128:] = dot_tn(
            grown_one[pair, :, :T], (ups_all[pair] * inverse[0, pair]).astype(BF16)
        )
    wide[:, :D] = head_back(unit_q[0], fact_q[0], grads[:, :D], ones).astype(BF16)
    back = dot(wide[:, :D], wqs_t[:D])
    mixed[0] = after[...].astype(F32) + dot(collect(3).astype(BF16), wob[:512])
    for index in (1, 2):
        for copy in near[index]:
            copy.wait_recv()
    for pair in range(PAIRS):
        for part in range(2):
            head = 2 * pair + part
            inverse_rim[pair, part * T : part * T + T] = jnp.broadcast_to(
                stats_rim[:, head : head + 1], (T, 128)
            )

    for index in range(3):
        for copy in near[index]:
            copy.wait_send()
    for phase in range(4):
        whole(phase).wait_send()
    far_whole.wait_recv()
    grad_att = dot(unpacked(got_rim[...]).astype(BF16), wos_t[...])
    ups_all = stacked_ups()
    dscore = [
        window_dscore(
            ups_all[pair],
            grown_rim[pair],
            attended_rim[:, lanes(pair)],
            values[pair, :T],
            inverse_rim[pair],
        )
        for pair in range(PAIRS)
    ]
    for pair in range(PAIRS):
        grads[:, D + pair * 128 : D + pair * 128 + 128] = partial[pair, :T, :128] + dot_tn(
            dscore[pair], queries[2, pair]
        )
        wide[:, 2 * D + pair * 128 : 2 * D + pair * 128 + 128] = (
            partial[pair, :T, 128:]
            + dot_tn(grown_rim[pair], (ups_all[pair] * inverse_rim[pair]).astype(BF16))
        ).astype(BF16)
    wide[:, D : 2 * D] = head_back(unit_k[0], fact_k[0], grads[:, D:], ones).astype(BF16)
    back = back + dot(wide[:, D:], wqs_t[D:])
    inputs = tok[...].astype(F32)
    fact_one = row_factor(inputs)
    mixed[0] += dot(collect(4).astype(BF16), wob[512:])
    grad[0] = grad_after + row_back(inputs * fact_one, fact_one, back)

    far_whole.wait_send()
    whole(4).wait_send()


def deliver(mixed, grad, mixed_hbm, grad_hbm, sem):
    copies = [
        pltpu.make_async_copy(
            source.at[0, pl.ds(part * 32, 32)],
            target.at[0, pl.ds(part * 32, 32)],
            sem.at[which, part],
        )
        for part in range(4)
        for which, (source, target) in enumerate(((mixed, mixed_hbm), (grad, grad_hbm)))
    ]
    for copy in copies:
        copy.start()
    for copy in copies:
        copy.wait()


def per_device(bands, spaces, *arrays):
    kept = pltpu.VMEM((1, T, D), F32)
    vmem = pl.BlockSpec(memory_space=pltpu.VMEM)
    hbm = pl.BlockSpec(memory_space=pltpu.HBM)
    out = jax.ShapeDtypeStruct((1, T, D), F32)
    count = T // bands
    dma = pltpu.SemaphoreType.DMA
    scratch = [
        pltpu.VMEM((T, D), BF16),
        pltpu.VMEM((T, D), BF16),
        pltpu.VMEM((T, D), BF16),
        pltpu.VMEM((3, bands, T), jnp.int32),
        pltpu.SMEM((HEADS,), F32),
        pltpu.SMEM((HEADS,), F32),
        pltpu.VMEM((D, 3 * D), BF16),
        pltpu.VMEM((D, D), BF16),
        pltpu.VMEM((D, 3 * D), BF16),
        pltpu.VMEM((D, D), BF16),
        pltpu.VMEM((3 * D, D), BF16),
        pltpu.VMEM((D, D), BF16),
        pltpu.VMEM((3 * D, D), BF16),
        pltpu.VMEM((2 * T, D), BF16),
        pltpu.VMEM((PAIRS, 2 * T, 256), BF16),
        pltpu.VMEM((T, D), BF16),
        pltpu.VMEM((PAIRS, T, 256), BF16),
        pltpu.VMEM((3, PAIRS, 2 * T, 128), BF16),
        pltpu.VMEM((PAIRS, 2 * T, 128), BF16),
        pltpu.VMEM((PAIRS, 2 * T, 2 * T), BF16),
        pltpu.VMEM((PAIRS, 2 * T, T), BF16),
        pltpu.VMEM((PAIRS, 2 * T, 256), F32),
        pltpu.VMEM((1, PAIRS, 2 * T, 128), F32),
        pltpu.VMEM((PAIRS, 2 * T, 128), F32),
        pltpu.VMEM((2, T, D), F32),
        pltpu.VMEM((2, T, D), F32),
        pltpu.VMEM((2, T, D), F32),
        pltpu.VMEM((2, T, D), F32),
        pltpu.VMEM((T, 3 * D), BF16),
        pltpu.VMEM((T, D), BF16),
        pltpu.VMEM((T, D), BF16),
        pltpu.VMEM((T, D), BF16),
        pltpu.VMEM((T, 128), F32),
        pltpu.VMEM((T, 128), F32),
        pltpu.VMEM((T, 2 * D), F32),
        pltpu.VMEM((3, bands, 2 * count, HALF), BF16),
        pltpu.VMEM((3, bands, 2 * count, HALF), BF16),
        pltpu.VMEM((bands, 2 * count, HALF), BF16),
        pltpu.VMEM((bands, 2 * count, 256), BF16),
        pltpu.VMEM((bands, 2 * count, 256), BF16),
        pltpu.VMEM((bands, 2 * count, 128), BF16),
        pltpu.VMEM((bands, 2 * count, 128), BF16),
        dma((11,)),
        dma((3, 2)),
        dma((3, 2)),
        dma((5,)),
        dma((5,)),
        dma,
        dma,
    ]
    made = pl.pallas_call(
        functools.partial(kernel, bands, spaces),
        out_shape=(kept, kept),
        in_specs=[hbm] * 9,
        out_specs=(vmem, vmem),
        scratch_shapes=scratch,
        compiler_params=pltpu.CompilerParams(
            collective_id=0, has_side_effects=True, vmem_limit_bytes=63 * 1024 * 1024
        ),
        cost_estimate=pl.CostEstimate(
            flops=3_500_000_000, bytes_accessed=11_000_000, transcendentals=600_000
        ),
    )(*arrays)
    return pl.pallas_call(
        deliver,
        out_shape=(out, out),
        in_specs=[vmem] * 2,
        out_specs=(hbm, hbm),
        scratch_shapes=[dma((2, 4))],
    )(*[pltpu.with_memory_space_constraint(part, pltpu.VMEM) for part in made])


def solution(mesh):
    cells = P("band", "space", None)
    return jax.shard_map(
        functools.partial(per_device, mesh.shape["band"], mesh.shape["space"]),
        mesh=mesh,
        in_specs=(cells, cells, P(), P(), P(), P(), P(), P(), P()),
        out_specs=(cells, cells),
        check_vma=False,
    )
```

```python
import functools

import jax
import jax.numpy as jnp
from jax import lax
from jax.experimental import pallas as pl
from jax.experimental.pallas import tpu as pltpu
from jax.sharding import PartitionSpec as P

D = 768
HALF = D // 2
HEADS = 12
HEAD_DIM = 64
PAIRS = HEADS // 2
T = 128
RADIUS = 64
EPS = 1e-06
MESH = pl.DeviceIdType.MESH
F32 = jnp.float32
BF16 = jnp.bfloat16


def dot(left, right):
    return jnp.dot(left, right, preferred_element_type=F32)


def dot_nt(left, right):
    return lax.dot_general(left, right, (((1,), (1,)), ((), ())), preferred_element_type=F32)


def dot_tn(left, right):
    return lax.dot_general(left, right, (((0,), (0,)), ((), ())), preferred_element_type=F32)


def row_factor(values):
    return lax.rsqrt(jnp.sum(values * values, axis=-1, keepdims=True) * (1.0 / D) + EPS)


def row_back(unit, factor, upstream):
    return factor * (upstream - unit * (jnp.sum(unit * upstream, axis=-1, keepdims=True) * (1.0 / D)))


def head_means(values, ones):
    low = values.astype(BF16)
    width = ones.shape[0]
    parts = [dot(low[:, at : at + width], ones) for at in range(0, values.shape[1], width)]
    return jnp.concatenate(parts, axis=1) * (1.0 / HEAD_DIM)


def head_factor(values, ones):
    return lax.rsqrt(head_means(values * values, ones) + EPS)


def head_back(unit, factor, upstream, ones):
    return factor * (upstream - unit * head_means(unit * upstream, ones))


def stacked(pair, low):
    return jnp.concatenate([jnp.where(low, pair, 0.0), jnp.where(low, 0.0, pair)], axis=0).astype(BF16)


def lanes(pair):
    return slice(pair * 128, pair * 128 + 128)


def paired(low, stack):
    return jnp.where(low, stack[:T], stack[T:])


def grown(query_stack, keys, mask):
    scores = jnp.exp(dot_nt(query_stack, keys))
    return jnp.concatenate([scores[:T] * mask, scores[T:] * mask], axis=0).astype(BF16)


def inner(ups, outs, values_one):
    return dot_nt(jnp.concatenate([ups, outs], axis=1), values_one)


def kernel(
    bands,
    spaces,
    tok_hbm,
    cot_hbm,
    vis_hbm,
    tau_space_hbm,
    tau_band_hbm,
    wqs_hbm,
    wos_hbm,
    wqb_hbm,
    wob_hbm,
    mixed,
    grad,
    tok,
    halo,
    cot,
    vis,
    tau_space,
    tau_band,
    wqs,
    wos,
    wqb,
    wob,
    wqs_t,
    wos_t,
    wqb_t,
    keys,
    values,
    keys_two,
    values_two,
    queries,
    ups_stack,
    grown_one,
    grown_rim,
    partial,
    inverse,
    inverse_rim,
    unit_q,
    fact_q,
    unit_k,
    fact_k,
    wide,
    after,
    attended,
    attended_rim,
    stats,
    stats_rim,
    grads,
    sent,
    got,
    got_rim,
    sent_far,
    sent_four,
    got_four,
    sent_two,
    got_two,
    local_sem,
    near_send,
    near_recv,
    all_send,
    all_recv,
    far_send,
    far_recv,
):
    band = lax.axis_index("band")
    space = lax.axis_index("space")
    count = T // bands
    chunk = lax.div(band, 2) + (bands // 2) * lax.rem(band, 2)
    right = lax.rem(space + 1, spaces)
    left = lax.rem(space + spaces - 1, spaces)

    def local(source, target, index):
        return pltpu.make_async_copy(source, target, local_sem.at[index])

    copies = {
        "tok": local(tok_hbm.at[0], tok, 0),
        "wqs": local(wqs_hbm, wqs, 1),
        "cot": local(cot_hbm.at[0], cot, 2),
        "wos": local(wos_hbm, wos, 3),
        "wob": local(wob_hbm, wob, 4),
        "wqb": local(wqb_hbm, wqb, 5),
        "tau_space": local(tau_space_hbm, tau_space, 9),
        "tau_band": local(tau_band_hbm, tau_band, 10),
    }
    for index, block in enumerate((left, space, right)):
        copies["vis%d" % index] = local(
            vis_hbm.at[:, pl.ds(pl.multiple_of(block * T, T), T)], vis.at[index], 6 + index
        )
    early = ("tok", "cot", "vis0", "vis1", "vis2", "tau_space", "tau_band", "wqs")
    late = ("wob", "wos", "wqb")
    for name in early:
        copies[name].start()

    barrier = pltpu.get_barrier_semaphore()
    for other in (left, right):
        pl.semaphore_signal(barrier, inc=1, device_id=(band, other), device_id_type=MESH)
    for step in range(1, bands):
        pl.semaphore_signal(
            barrier,
            inc=1,
            device_id=(lax.rem(band + step, bands), space),
            device_id_type=MESH,
        )
    pl.semaphore_wait(barrier, bands + 1)

    def neighbours(source, target, index):
        return [
            pltpu.make_async_remote_copy(
                src_ref=source.at[pl.ds(at, RADIUS)],
                dst_ref=target.at[pl.ds(at, RADIUS)],
                send_sem=near_send.at[index, side],
                recv_sem=near_recv.at[index, side],
                device_id=(band, other),
                device_id_type=MESH,
            )
            for side, at, other in ((0, RADIUS, right), (1, 0, left))
        ]

    near = [
        neighbours(tok, halo, 0),
        neighbours(attended, attended_rim, 1),
        neighbours(stats, stats_rim, 2),
    ]
    copies["tok"].wait()
    for copy in near[0]:
        copy.start()

    outbox = [sent.at[0], sent.at[1], sent.at[2], sent_four, sent_two]
    inbox = [got.at[0], got.at[1], got.at[2], got_four, got_two]

    farthest_first = sorted(range(1, bands), key=lambda step: abs(step - bands // 2))

    def exchange(phase, step):
        other = lax.rem(band + step, bands)
        away = lax.div(other, 2) + (bands // 2) * lax.rem(other, 2)
        return pltpu.make_async_remote_copy(
            src_ref=outbox[phase].at[away if phase < 2 else other],
            dst_ref=inbox[phase].at[band if phase < 2 else chunk],
            send_sem=all_send.at[phase],
            recv_sem=all_recv.at[phase],
            device_id=(other, space),
            device_id_type=MESH,
        )

    def whole(phase):
        return pltpu.make_async_remote_copy(
            src_ref=outbox[phase].at[pl.ds(0, bands - 1)],
            dst_ref=inbox[phase].at[pl.ds(0, bands - 1)],
            send_sem=all_send.at[phase],
            recv_sem=all_recv.at[phase],
            device_id=(lax.rem(band + 1, bands), space),
            device_id_type=MESH,
        )

    def packed(rows):
        half = rows.shape[1] // 2
        pieces = [
            rows[:, :half].reshape(bands, count, half),
            rows[:, half:].reshape(bands, count, half),
        ]
        return jnp.concatenate(pieces, axis=1).astype(BF16)

    def scatter(phase, rows):
        outbox[phase][...] = packed(rows)
        for step in farthest_first:
            exchange(phase, step).start()
        if phase < 2:
            inbox[phase][band] = outbox[phase][chunk]
        else:
            inbox[phase][chunk] = outbox[phase][band]

    def unpacked(slots):
        rows = slots.astype(F32)
        half = rows.shape[2]
        return jnp.concatenate(
            [rows[:, :count].reshape(T, half), rows[:, count:].reshape(T, half)], axis=1
        )

    def collect(phase):
        whole(phase).wait_recv()
        return unpacked(inbox[phase][...])

    toward = lax.rem(space + spaces - 1 + 2 * lax.rem(band, 2), spaces)

    def far(step):
        other = lax.rem(band + step, bands)
        return pltpu.make_async_remote_copy(
            src_ref=sent_far.at[other],
            dst_ref=got_rim.at[chunk],
            send_sem=far_send,
            recv_sem=far_recv,
            device_id=(other, toward),
            device_id_type=MESH,
        )

    far_whole = pltpu.make_async_remote_copy(
        src_ref=sent_far,
        dst_ref=got_rim,
        send_sem=far_send,
        recv_sem=far_recv,
        device_id=(band, toward),
        device_id_type=MESH,
    )

    low = lax.broadcasted_iota(jnp.int32, (T, 128), 1) < HEAD_DIM
    ones = jnp.where(
        (lax.broadcasted_iota(jnp.int32, (256, 256), 0) >> 6)
        == (lax.broadcasted_iota(jnp.int32, (256, 256), 1) >> 6),
        1.0,
        0.0,
    ).astype(BF16)
    for pair in range(PAIRS):
        values[pair, :, 128:] = jnp.ones((2 * T, 128), BF16)
        values_two[pair, :, 128:] = jnp.ones((T, 128), BF16)

    for index in range(3):
        copies["vis%d" % index].wait()
    group = lax.broadcasted_iota(jnp.int32, (bands, 128), 0)
    lane = lax.broadcasted_iota(jnp.int32, (bands, 128), 1)

    def own_row(index):
        return jnp.sum(jnp.where(group == band, vis[index], 0), axis=0, keepdims=True)

    row = lax.broadcasted_iota(jnp.int32, (T, T), 0)
    col = lax.broadcasted_iota(jnp.int32, (T, T), 1)
    own_seen = own_row(1) == 1
    rim_seen = jnp.where(lane[:1] < RADIUS, own_row(2), own_row(0)) == 1

    def within(offset):
        return (offset >= -RADIUS) & (offset <= RADIUS)

    def flag(test):
        return jnp.where(test, 1.0, 0.0)

    mask_own = flag(within(row - col) & (own_seen | (row == col)))
    mask_rim = flag(within(jnp.where(col < RADIUS, col + T, col - T) - row) & rim_seen)
    mask_back = flag(within(jnp.where(row < RADIUS, row + T, row - T) - col) & own_seen)
    pick = flag(row == chunk * count + lax.rem(col, count))
    spread = dot(vis[1].astype(F32), pick)
    seen = jnp.sum(
        jnp.where(group == lax.div(lane, count), spread, 0.0), axis=0, keepdims=True
    )
    same = lax.rem(row, count) == lax.rem(col, count)
    mask_two = flag(same & ((seen > 0.5) | (row == col)))

    copies["tau_space"].wait()
    copies["tau_band"].wait()

    def scale_row(tau):
        pieces = [
            jnp.where(low[:1], tau[2 * pair], tau[2 * pair + 1]) * (1.0 / HEAD_DIM)
            for pair in range(PAIRS)
        ]
        return jnp.concatenate(pieces, axis=1)

    scale_space = scale_row(tau_space)
    scale_band = scale_row(tau_band)

    def put_queries(slot, unit, scale):
        scaled = unit * scale
        for pair in range(PAIRS):
            queries[slot, pair] = stacked(scaled[:, lanes(pair)], low)

    def normed_heads(normed, weight, slot, which):
        raw = dot(normed, weight)
        factor = head_factor(raw, ones)
        unit = raw * factor
        if which is not None:
            which[0][slot] = unit
            which[1][slot] = factor
        return unit

    inputs = tok[...].astype(F32)
    normed = (inputs * row_factor(inputs)).astype(BF16)
    copies["wqs"].wait()
    for name in late:
        copies[name].start()
    put_queries(0, normed_heads(normed, wqs[:, :D], 0, (unit_q, fact_q)), scale_space)
    keys[:T] = normed_heads(normed, wqs[:, D : 2 * D], 0, (unit_k, fact_k)).astype(BF16)
    raw = dot(normed, wqs[:, 2 * D :]).astype(BF16)
    for pair in range(PAIRS):
        values[pair, :T, :128] = raw[:, lanes(pair)]
    for pair in range(PAIRS):
        grown_one[pair, :, :T] = grown(queries[0, pair], keys[:T, lanes(pair)], mask_own)
    for pair in range(PAIRS):
        partial[pair] = dot(grown_one[pair, :, :T], values[pair, :T])

    copies["cot"].wait()
    scatter(0, cot[...].astype(F32))

    for copy in near[0]:
        copy.wait_recv()
    rim = halo[...].astype(F32)
    normed = (rim * row_factor(rim)).astype(BF16)
    keys[T:] = normed_heads(normed, wqs[:, D : 2 * D], None, None).astype(BF16)
    raw = dot(normed, wqs[:, 2 * D :]).astype(BF16)
    for pair in range(PAIRS):
        values[pair, T:, :128] = raw[:, lanes(pair)]
    for pair in range(PAIRS):
        grown_one[pair, :, T:] = grown(queries[0, pair], keys[T:, lanes(pair)], mask_rim)
    for pair in range(PAIRS):
        out = partial[pair] + dot(grown_one[pair, :, T:], values[pair, T:])
        turned = 1.0 / out[:, 128:]
        inverse[0, pair] = turned
        attended[:, lanes(pair)] = paired(low, out[:, :128] * turned).astype(BF16)
    copies["wos"].wait()
    after[...] = (inputs + dot(attended[...], wos[...])).astype(BF16)
    scatter(1, after[...].astype(F32))
    table = jnp.zeros((T, 128), F32)
    for pair in range(PAIRS):
        table = jnp.where(col == 2 * pair, inverse[0, pair, :T], table)
        table = jnp.where(col == 2 * pair + 1, inverse[0, pair, T:], table)
    stats[...] = table

    upstream = collect(0)
    copies["wob"].wait()
    grad_att = dot_nt(upstream.astype(BF16), wob[...])
    for pair in range(PAIRS):
        ups_stack[pair] = stacked(grad_att[:, lanes(pair)], low)
    put_queries(2, normed_heads(normed, wqs[:, :D], None, None), scale_space)
    copies["wqb"].wait()
    for at in range(0, 3 * D, 256):
        wqb_t[at : at + 256] = wqb[:, at : at + 256].T

    for at in range(0, D, 256):
        wos_t[at : at + 256] = wos[:, at : at + 256].T
    for index in (1, 2):
        for copy in near[index]:
            copy.start()
    rows = collect(1)
    fact_two = row_factor(rows)
    unit_two = rows * fact_two
    normed = unit_two.astype(BF16)
    put_queries(1, normed_heads(normed, wqb[:, :D], 1, (unit_q, fact_q)), scale_band)
    keys_two[...] = normed_heads(normed, wqb[:, D : 2 * D], 1, (unit_k, fact_k)).astype(BF16)
    raw = dot(normed, wqb[:, 2 * D :]).astype(BF16)
    for pair in range(PAIRS):
        values_two[pair, :, :128] = raw[:, lanes(pair)]
    everyone = range(PAIRS)
    weight = [grown(queries[1, p], keys_two[:, lanes(p)], mask_two) for p in everyone]
    outs, turned = [], []
    for pair in everyone:
        out = dot(weight[pair], values_two[pair])
        turned.append(1.0 / out[:, 128:])
        outs.append(out[:, :128] * turned[pair])
    scatter(3, jnp.concatenate([paired(low, out) for out in outs[:4]], axis=1))
    dscore = []
    for pair in everyone:
        ups = ups_stack[pair]
        inside = inner(ups, (-ups.astype(F32) * outs[pair]).astype(BF16), values_two[pair])
        dscore.append((weight[pair].astype(F32) * (inside * turned[pair])).astype(BF16))
    for pair in everyone:
        at = lanes(pair)
        grads[:, at] = paired(low, dot(dscore[pair], keys_two[:, at])) * scale_band[:, at]
        grads[:, D + pair * 128 : D + pair * 128 + 128] = dot_tn(dscore[pair], queries[1, pair])
        wide[:, 2 * D + pair * 128 : 2 * D + pair * 128 + 128] = dot_tn(
            weight[pair], (ups_stack[pair].astype(F32) * turned[pair]).astype(BF16)
        ).astype(BF16)
    wide[:, :D] = head_back(unit_q[1], fact_q[1], grads[:, :D], ones).astype(BF16)
    wide[:, D : 2 * D] = head_back(unit_k[1], fact_k[1], grads[:, D:], ones).astype(BF16)
    back = dot(wide[...], wqb_t[...])
    grad_after = upstream + row_back(unit_two, fact_two, back)
    scatter(2, grad_after)
    sent_far[...] = packed(dot(grad_after.astype(BF16), wos_t[...]))
    for step in farthest_first + [0]:
        far(step).start()
    scatter(4, jnp.concatenate([paired(low, out) for out in outs[4:]], axis=1))

    for at in range(0, 3 * D, 256):
        wqs_t[at : at + 256] = wqs[:, at : at + 256].T
    for pair in range(PAIRS):
        grown_rim[pair] = grown(queries[2, pair], keys[:T, lanes(pair)], mask_back)

    grad_after = collect(2)
    grad_att = dot(grad_after.astype(BF16), wos_t[...])
    def stacked_ups():
        return [
            jnp.concatenate(
                [jnp.where(low, part, 0.0), jnp.where(low, 0.0, part)], axis=0
            )
            for part in (grad_att[:, lanes(pair)] for pair in range(PAIRS))
        ]

    def window_dscore(ups, weight, outs, value, turned):
        out = jnp.concatenate([outs, outs], axis=0).astype(F32)
        inside = inner(ups.astype(BF16), (-ups * out).astype(BF16), value)
        return (weight.astype(F32) * (inside * turned)).astype(BF16)

    ups_all = stacked_ups()
    dscore = []
    for pair in range(PAIRS):
        turned = inverse[0, pair]
        turned = jnp.concatenate([turned, turned], axis=1)
        dscore.append(
            window_dscore(
                ups_all[pair], grown_one[pair], attended[:, lanes(pair)], values[pair], turned
            )
        )
    for pair in range(PAIRS):
        at = lanes(pair)
        grads[:, at] = paired(low, dot(dscore[pair], keys[:, at])) * scale_space[:, at]
        partial[pair, :T, :128] = dot_tn(dscore[pair][:, :T], queries[0, pair])
        partial[pair, :T, 128:] = dot_tn(
            grown_one[pair, :, :T], (ups_all[pair] * inverse[0, pair]).astype(BF16)
        )
    wide[:, :D] = head_back(unit_q[0], fact_q[0], grads[:, :D], ones).astype(BF16)
    back = dot(wide[:, :D], wqs_t[:D])
    mixed[0] = after[...].astype(F32) + dot(collect(3).astype(BF16), wob[:512])
    for index in (1, 2):
        for copy in near[index]:
            copy.wait_recv()
    for pair in range(PAIRS):
        for part in range(2):
            head = 2 * pair + part
            inverse_rim[pair, part * T : part * T + T] = jnp.broadcast_to(
                stats_rim[:, head : head + 1], (T, 128)
            )

    for index in range(3):
        for copy in near[index]:
            copy.wait_send()
    for phase in range(4):
        whole(phase).wait_send()
    far_whole.wait_recv()
    grad_att = unpacked(got_rim[...])
    ups_all = stacked_ups()
    dscore = [
        window_dscore(
            ups_all[pair],
            grown_rim[pair],
            attended_rim[:, lanes(pair)],
            values[pair, :T],
            inverse_rim[pair],
        )
        for pair in range(PAIRS)
    ]
    for pair in range(PAIRS):
        grads[:, D + pair * 128 : D + pair * 128 + 128] = partial[pair, :T, :128] + dot_tn(
            dscore[pair], queries[2, pair]
        )
        wide[:, 2 * D + pair * 128 : 2 * D + pair * 128 + 128] = (
            partial[pair, :T, 128:]
            + dot_tn(grown_rim[pair], (ups_all[pair] * inverse_rim[pair]).astype(BF16))
        ).astype(BF16)
    wide[:, D : 2 * D] = head_back(unit_k[0], fact_k[0], grads[:, D:], ones).astype(BF16)
    back = back + dot(wide[:, D:], wqs_t[D:])
    inputs = tok[...].astype(F32)
    fact_one = row_factor(inputs)
    mixed[0] += dot(collect(4).astype(BF16), wob[512:])
    grad[0] = grad_after + row_back(inputs * fact_one, fact_one, back)

    far_whole.wait_send()
    whole(4).wait_send()


def deliver(mixed, grad, mixed_hbm, grad_hbm, sem):
    copies = [
        pltpu.make_async_copy(
            source.at[0, pl.ds(part * 32, 32)],
            target.at[0, pl.ds(part * 32, 32)],
            sem.at[which, part],
        )
        for part in range(4)
        for which, (source, target) in enumerate(((mixed, mixed_hbm), (grad, grad_hbm)))
    ]
    for copy in copies:
        copy.start()
    for copy in copies:
        copy.wait()


def per_device(bands, spaces, *arrays):
    kept = pltpu.VMEM((1, T, D), F32)
    vmem = pl.BlockSpec(memory_space=pltpu.VMEM)
    hbm = pl.BlockSpec(memory_space=pltpu.HBM)
    out = jax.ShapeDtypeStruct((1, T, D), F32)
    count = T // bands
    dma = pltpu.SemaphoreType.DMA
    scratch = [
        pltpu.VMEM((T, D), BF16),
        pltpu.VMEM((T, D), BF16),
        pltpu.VMEM((T, D), BF16),
        pltpu.VMEM((3, bands, T), jnp.int32),
        pltpu.SMEM((HEADS,), F32),
        pltpu.SMEM((HEADS,), F32),
        pltpu.VMEM((D, 3 * D), BF16),
        pltpu.VMEM((D, D), BF16),
        pltpu.VMEM((D, 3 * D), BF16),
        pltpu.VMEM((D, D), BF16),
        pltpu.VMEM((3 * D, D), BF16),
        pltpu.VMEM((D, D), BF16),
        pltpu.VMEM((3 * D, D), BF16),
        pltpu.VMEM((2 * T, D), BF16),
        pltpu.VMEM((PAIRS, 2 * T, 256), BF16),
        pltpu.VMEM((T, D), BF16),
        pltpu.VMEM((PAIRS, T, 256), BF16),
        pltpu.VMEM((3, PAIRS, 2 * T, 128), BF16),
        pltpu.VMEM((PAIRS, 2 * T, 128), BF16),
        pltpu.VMEM((PAIRS, 2 * T, 2 * T), BF16),
        pltpu.VMEM((PAIRS, 2 * T, T), BF16),
        pltpu.VMEM((PAIRS, 2 * T, 256), F32),
        pltpu.VMEM((1, PAIRS, 2 * T, 128), F32),
        pltpu.VMEM((PAIRS, 2 * T, 128), F32),
        pltpu.VMEM((2, T, D), F32),
        pltpu.VMEM((2, T, D), F32),
        pltpu.VMEM((2, T, D), F32),
        pltpu.VMEM((2, T, D), F32),
        pltpu.VMEM((T, 3 * D), BF16),
        pltpu.VMEM((T, D), BF16),
        pltpu.VMEM((T, D), BF16),
        pltpu.VMEM((T, D), BF16),
        pltpu.VMEM((T, 128), F32),
        pltpu.VMEM((T, 128), F32),
        pltpu.VMEM((T, 2 * D), F32),
        pltpu.VMEM((3, bands, 2 * count, HALF), BF16),
        pltpu.VMEM((3, bands, 2 * count, HALF), BF16),
        pltpu.VMEM((bands, 2 * count, HALF), BF16),
        pltpu.VMEM((bands, 2 * count, HALF), BF16),
        pltpu.VMEM((bands, 2 * count, 256), BF16),
        pltpu.VMEM((bands, 2 * count, 256), BF16),
        pltpu.VMEM((bands, 2 * count, 128), BF16),
        pltpu.VMEM((bands, 2 * count, 128), BF16),
        dma((11,)),
        dma((3, 2)),
        dma((3, 2)),
        dma((5,)),
        dma((5,)),
        dma,
        dma,
    ]
    made = pl.pallas_call(
        functools.partial(kernel, bands, spaces),
        out_shape=(kept, kept),
        in_specs=[hbm] * 9,
        out_specs=(vmem, vmem),
        scratch_shapes=scratch,
        compiler_params=pltpu.CompilerParams(
            collective_id=0, has_side_effects=True, vmem_limit_bytes=63 * 1024 * 1024
        ),
        cost_estimate=pl.CostEstimate(
            flops=3_500_000_000, bytes_accessed=11_000_000, transcendentals=600_000
        ),
    )(*arrays)
    return pl.pallas_call(
        deliver,
        out_shape=(out, out),
        in_specs=[vmem] * 2,
        out_specs=(hbm, hbm),
        scratch_shapes=[dma((2, 4))],
    )(*[pltpu.with_memory_space_constraint(part, pltpu.VMEM) for part in made])


def solution(mesh):
    cells = P("band", "space", None)
    return jax.shard_map(
        functools.partial(per_device, mesh.shape["band"], mesh.shape["space"]),
        mesh=mesh,
        in_specs=(cells, cells, P(), P(), P(), P(), P(), P(), P()),
        out_specs=(cells, cells),
        check_vma=False,
    )
```
